32 devices in a mesh: ctx: 4 (over x, core), fsdp: 4 (over z), batch: 2 (over y).
Axes of the slice: x: 2, y: 2, z: 4, core: 2. Of those that a mesh axis runs over, the one named last changes fastest.
Arguments:
- inputs: bfloat16 [2, 512, 4096], P('batch', 'ctx'), may hold values from -6 to 6
- values: bfloat16 [2, 512, 2048], P('batch', 'ctx', 'fsdp'), may hold values from -6 to 6
- w_qk: bfloat16 [4096, 256], P('fsdp'), may hold values from -0.09375 to 0.09375
- conv_qk: float32 [3, 256], P(None, 'fsdp'), may hold values from -3 to 3
- conv_v: float32 [3, 2048], P(None, 'fsdp'), may hold values from -3 to 3
- d_attn: bfloat16 [2, 512, 2048], P('batch', 'ctx', 'fsdp'), may hold values from -6 to 6
Outputs:
- attended: bfloat16 [2, 512, 2048], P('batch', 'ctx', 'fsdp')
- grad_v: bfloat16 [2, 512, 2048], P('batch', 'ctx', 'fsdp')
- grad_w: float32 [4096, 256], P(('ctx', 'batch'), 'fsdp')
The draws below stay inside these ranges and needn't reach their ends.
All inputs are finite; a program needn't handle non-finite values.
Results may differ from the reference program's by a relative error of at most 0.013.
Values may be sent and summed in bfloat16 or wider, within the bound.
A program may use at most 64 MiB of HBM per device.

```python
import jax
import jax.numpy as jnp
from jax import lax

D = 4096
H = 8
F = 16
E = 256
CONV = 3
TOK_DEV = 128
QK = 256
V = 2048
SEQS = 2
LENGTH = 512
N_CTX = 4


def steps_of(own_key, extent, split, smallest, high):
    gain = 1.0
    for position, blocks in split:
        heights = jax.random.uniform(jax.random.fold_in(jax.random.fold_in(own_key, 6), position), (blocks,), jnp.float32, smallest / len(split), high / len(split))
        gain = gain * jnp.repeat(jnp.exp(heights), extent[position] // blocks).reshape((-1,) + (1,) * (len(extent) - 1 - position))
    return gain


def centred(rng, shape, scale, reach, split=(), dtype=jnp.bfloat16):
    level = steps_of(rng, shape, split, -0.22, 0.18) if split else 1.0
    result = jax.random.normal(rng, shape, jnp.float32) * scale * level
    return jnp.minimum(jnp.maximum(result, -reach), reach).astype(dtype)


def setup_inputs(seed: int = 0) -> dict:
    streams_of = jax.random.split(jax.random.key(seed), 7)
    return {
        "inputs": centred(streams_of[0], (SEQS, LENGTH, D), 1.0, 6.0, ((0, 2), (1, 4))),
        "values": centred(streams_of[1], (SEQS, LENGTH, V), 1.0, 6.0, ((0, 2), (1, 4), (2, 4))),
        "w_qk": centred(streams_of[2], (D, QK), D ** -0.5, 0.09375, ((0, 4),)),
        "conv_qk": centred(streams_of[3], (CONV, QK), 0.6, 3.0, ((1, 4),), jnp.float32),
        "conv_v": centred(streams_of[4], (CONV, V), 0.6, 3.0, ((1, 4),), jnp.float32),
        "d_attn": centred(streams_of[5], (SEQS, LENGTH, V), 1.0, 6.0, ((0, 2), (1, 4), (2, 4))),
    }


eps_norm = 1e-05
highest = lax.Precision.HIGHEST

def rounded(array):
    return lax.optimization_barrier(array.astype(jnp.bfloat16)).astype(jnp.float32)

def features(vector):
    leading = vector.shape[:-1]
    quadratic = (vector[..., :, None] * vector[..., None, :]).reshape(leading + (F * F,))
    constant = jnp.ones(leading + (1,), jnp.float32)
    return jnp.concatenate([constant, vector * F ** (-0.25), quadratic * (2.0 * F) ** (-0.5)], axis=-1)

def features_back(vector, upstream):
    leading = vector.shape[:-1]
    linear = upstream[..., 1:1 + F]
    square = upstream[..., 1 + F:].reshape(leading + (F, F))
    paired = lax.optimization_barrier(jnp.sum(square * vector[..., None, :], axis=-1)) + lax.optimization_barrier(jnp.sum(square * vector[..., :, None], axis=-2))
    return linear * F ** (-0.25) + paired * (2.0 * F) ** (-0.5)

def split_heads(block):
    paired = block[..., :QK].reshape(block.shape[:-1] + (H, 2 * F)).astype(jnp.float32)
    queries = paired[..., :F]
    key_rows = paired[..., F:]
    valued = block[..., QK:].reshape(block.shape[:-1] + (H, E)).astype(jnp.float32)
    return (queries, key_rows, valued)

def block_kernel(queries, key_rows):
    dotted = jnp.einsum('sthf,sphf->shtp', queries, key_rows) * F ** (-0.5)
    rows_at = lax.broadcasted_iota(jnp.int32, (TOK_DEV, TOK_DEV), 0)
    cols_at = lax.broadcasted_iota(jnp.int32, (TOK_DEV, TOK_DEV), 1)
    causal = (cols_at <= rows_at)[None, None]
    kernel = jnp.where(causal, 1.0 + dotted + 0.5 * dotted * dotted, 0.0)
    return (dotted, causal, kernel)

def to_blocks(array):
    return array.reshape(SEQS, N_CTX, TOK_DEV, array.shape[-1]).transpose(1, 0, 2, 3)

def from_blocks(array):
    return array.transpose(1, 0, 2, 3).reshape(SEQS, LENGTH, array.shape[-1])

def local_state(block):
    queries, key_rows, valued = split_heads(block)
    return jnp.einsum('sphf,sphe->sfhe', features(key_rows), valued, precision=highest)

def forward_block(operands):
    block, prior, upstream = operands
    queries, key_rows, valued = split_heads(block)
    dotted, causal, kernel = block_kernel(queries, key_rows)
    kernel_b = rounded(kernel)
    mixed_out = jnp.einsum('shtp,sphe->sthe', kernel_b, valued)
    mixed_out = mixed_out + jnp.einsum('sthf,sfhe->sthe', features(queries), prior, precision=highest)
    scale_inv = lax.rsqrt(lax.optimization_barrier(jnp.mean(mixed_out * mixed_out, axis=-1, keepdims=True)) + eps_norm)
    normed = mixed_out * scale_inv
    attended = normed.astype(jnp.bfloat16).reshape(SEQS, TOK_DEV, V)
    grad_in = upstream.astype(jnp.float32).reshape(SEQS, TOK_DEV, H, E)
    d_mixed = (scale_inv * (grad_in - normed * lax.optimization_barrier(jnp.mean(grad_in * normed, axis=-1, keepdims=True)))).astype(jnp.bfloat16)
    d_state = jnp.einsum('sthf,sthe->sfhe', features(queries), d_mixed.astype(jnp.float32), precision=highest)
    return (attended, d_mixed, d_state)

def backward_block(operands):
    block, prior, later, d_mixed = operands
    queries, key_rows, valued = split_heads(block)
    dotted, causal, kernel = block_kernel(queries, key_rows)
    kernel_b = rounded(kernel)
    d_mixed32 = d_mixed.astype(jnp.float32)
    d_kernel = jnp.einsum('sthe,sphe->shtp', d_mixed32, valued)
    d_score = rounded(jnp.where(causal, d_kernel * (1.0 + dotted), 0.0) * F ** (-0.5))
    d_query = jnp.einsum('shtp,sphf->sthf', d_score, key_rows)
    d_query = d_query + features_back(queries, jnp.einsum('sthe,sfhe->sthf', d_mixed32, prior, precision=highest))
    d_key = jnp.einsum('shtp,sthf->sphf', d_score, queries)
    d_key = d_key + features_back(key_rows, jnp.einsum('sphe,sfhe->sphf', valued, later, precision=highest))
    d_valued = jnp.einsum('shtp,sthe->sphe', kernel_b, d_mixed32)
    d_valued = d_valued + jnp.einsum('sphf,sfhe->sphe', features(key_rows), later, precision=highest)
    d_paired = jnp.concatenate([d_query, d_key], axis=-1).reshape(SEQS, TOK_DEV, QK)
    return jnp.concatenate([d_paired, d_valued.reshape(SEQS, TOK_DEV, V)], axis=-1)

def reference(inputs, values, w_qk, conv_qk, conv_v, d_attn):
    conv_w = jnp.concatenate([conv_qk, conv_v], axis=1)
    qk_raw = jnp.dot(inputs.reshape(SEQS * LENGTH, D), w_qk, preferred_element_type=jnp.float32)
    qk_raw = qk_raw.astype(jnp.bfloat16).reshape(SEQS, LENGTH, QK)
    joined = jnp.concatenate([qk_raw, values], axis=-1)
    running = jnp.zeros(joined.shape, jnp.float32)
    for offset in range(CONV):
        moved = jnp.pad(joined, ((0, 0), (offset, 0), (0, 0)))[:, :LENGTH, :]
        running = running + conv_w[offset] * moved.astype(jnp.float32)
    convolved = to_blocks(running.astype(jnp.bfloat16))
    upstream = to_blocks(d_attn)
    states = lax.map(local_state, convolved)
    zero_state = jnp.zeros((1,) + states.shape[1:], jnp.float32)
    prefix = jnp.concatenate([zero_state, jnp.cumsum(states, axis=0)[:-1]], axis=0)
    attended, d_mixed, d_states = lax.map(forward_block, (convolved, prefix, upstream))
    from_end = jnp.flip(jnp.cumsum(jnp.flip(d_states, axis=0), axis=0), axis=0)
    suffix = jnp.concatenate([from_end[1:], zero_state], axis=0)
    d_joined = from_blocks(lax.map(backward_block, (convolved, prefix, suffix, d_mixed)))
    running = jnp.zeros(d_joined.shape, jnp.float32)
    for offset in range(CONV):
        moved = jnp.pad(d_joined, ((0, 0), (0, offset), (0, 0)))[:, offset:, :]
        running = running + conv_w[offset] * moved
    grad_v = running[..., QK:].astype(jnp.bfloat16)
    d_qk = running[..., :QK].astype(jnp.bfloat16)
    grad_w = lax.dot_general(inputs.reshape(SEQS * LENGTH, D), d_qk.reshape(SEQS * LENGTH, QK), (((0,), (0,)), ((), ())), preferred_element_type=jnp.float32)
    grad_w = grad_w * (SEQS * LENGTH) ** (-0.5)
    attended = from_blocks(attended)
    return (attended, grad_v, grad_w)
```

```python
import functools

import jax
import jax.numpy as jnp
from jax import lax
from jax.experimental import pallas as pl
from jax.experimental.pallas import tpu as pltpu
from jax.sharding import PartitionSpec as P

F = 16
E = 256
CONV = 3
PACKED = 8 * F + F // 2 + 8 + F
RIM_V = 16
RIM = 8

eps_norm = 1e-05
MESH = pl.DeviceIdType.MESH
bf16, f32 = jnp.bfloat16, jnp.float32


def dot(a, b):
    return jnp.dot(a, b, preferred_element_type=f32)


def dot_nt(a, b):
    return lax.dot_general(a, b, (((1,), (1,)), ((), ())), preferred_element_type=f32)


def turned(rows, by):
    if by == 0:
        return rows
    return jnp.concatenate([rows[by:], rows[:by]], axis=0)


def features(vec):
    positions = vec.shape[1]
    rows = [vec * vec * (2.0 * F) ** (-0.5)]
    scaled = vec * F ** (-0.5)
    for by in range(1, F // 2):
        rows.append(scaled * turned(vec, by))
    rows.append(scaled[: F // 2] * vec[F // 2 :])
    first = lax.broadcasted_iota(jnp.int32, (8, positions), 0) == 0
    rows.append(jnp.where(first, 1.0, 0.0).astype(f32))
    rows.append(vec * F ** (-0.25))
    return jnp.concatenate(rows, axis=0)


def features_back(vec, up):
    half = F // 2
    total = vec * up[:F] * (2.0 * (2.0 * F) ** (-0.5))
    total = total + up[8 * F + half + 8 :] * F ** (-0.25)
    pairs = jnp.zeros_like(vec)
    for by in range(1, half):
        part = up[by * F : (by + 1) * F]
        pairs = pairs + turned(vec, by) * part + turned(vec * part, F - by)
    part = up[half * F : half * F + half]
    pairs = pairs + jnp.concatenate([vec[half:] * part, vec[:half] * part], axis=0)
    return total + pairs * F ** (-0.5)


def column_of(row):
    n = row.shape[1]
    same = lax.broadcasted_iota(jnp.int32, (n, n), 0) == lax.broadcasted_iota(jnp.int32, (n, n), 1)
    return jnp.sum(jnp.where(same, row, 0.0), axis=1, keepdims=True)


def body(
    dims, tokens, values, weights, conv_qk, conv_v, d_attn,
    attended, grad_v, grad_w,
    part_t, part_in, rim_out, rim_in, rim_t, vrim_in, ext_v, conv_b,
    state_out, state_in, prior, grad_out, grad_in, later, mixed_b,
    dv_ext, dqk_out, dqk_in, x_in, dq_all,
    part_ss, part_rs, rim_ss, rim_rs, vrim_ss, vrim_rs, state_ss, state_rs,
    grad_ss, grad_rs, dv_ss, dv_rs, dqk_ss, dqk_rs, x_ss, x_rs, dq_ss, dq_rs,
):
    n_ctx, n_fsdp, n_batch, gather = dims
    ctx, fsdp, batch = lax.axis_index("ctx"), lax.axis_index("fsdp"), lax.axis_index("batch")
    positions = tokens.shape[0]
    depth = weights.shape[0]
    width = conv_qk.shape[1]
    heads = width // (2 * F)
    wide = values.shape[1]
    group = n_ctx * n_batch
    me = ctx * n_batch + batch
    inner, outer = ctx > 0, ctx < n_ctx - 1

    def copy(src, dst, ss, rs, to):
        return pltpu.make_async_remote_copy(
            src_ref=src, dst_ref=dst, send_sem=ss, recv_sem=rs, device_id=to, device_id_type=MESH
        )

    bar = pltpu.get_barrier_semaphore()

    def greet(to):
        pl.semaphore_signal(bar, inc=1, device_id=to, device_id_type=MESH)

    for r in range(1, n_fsdp):
        greet((ctx, lax.rem(fsdp + r, n_fsdp), batch))
    if gather:
        for r in range(1, group):
            peer = lax.rem(me + r, group)
            greet((peer // n_batch, fsdp, lax.rem(peer, n_batch)))
        count = group - 1 + n_fsdp - 1
        same = range(1, n_fsdp)
    else:
        for r in range(1, n_ctx):
            greet((lax.rem(ctx + r, n_ctx), fsdp, batch))
        count = n_ctx - 1 + n_fsdp - 1
        same = range(1, n_fsdp)

    @pl.when(inner)
    def _():
        for r in same:
            greet((ctx - 1, lax.rem(fsdp + r, n_fsdp), batch))

    @pl.when(outer)
    def _():
        for r in same:
            greet((ctx + 1, lax.rem(fsdp + r, n_fsdp), batch))

    columns = pl.ds(pl.multiple_of(fsdp * depth, depth), depth)
    part = dot(tokens[:, columns], weights[...])
    part_t[...] = part.T.reshape(part_t.shape)
    rim_out[...] = part[positions - RIM :]
    pl.semaphore_wait(
        bar, count + jnp.where(inner, n_fsdp - 1, 0) + jnp.where(outer, n_fsdp - 1, 0)
    )

    def part_copy(r):
        peer = lax.rem(fsdp + r, n_fsdp)
        return copy(part_t.at[peer], part_in.at[fsdp], part_ss.at[r], part_rs.at[fsdp], (ctx, peer, batch))

    def rim_copy(r):
        peer = lax.rem(fsdp + r, n_fsdp)
        return copy(rim_out, rim_in.at[fsdp], rim_ss.at[r], rim_rs.at[fsdp], (ctx + 1, peer, batch))

    def vrim_copy():
        return copy(values.at[pl.ds(positions - RIM_V, RIM_V)], vrim_in, vrim_ss, vrim_rs, (ctx + 1, fsdp, batch))

    for r in range(1, n_fsdp):
        part_copy(r).start()

    @pl.when(outer)
    def _():
        for r in range(n_fsdp):
            rim_copy(r).start()
        vrim_copy().start()

    cols = grad_w.shape[1]

    def x_copy(r):
        peer = lax.rem(me + r, group)
        return copy(
            tokens.at[:, pl.ds(pl.multiple_of(peer * cols, cols), cols)],
            x_in.at[me], x_ss.at[r], x_rs.at[me],
            (peer // n_batch, fsdp, lax.rem(peer, n_batch)),
        )

    if gather:
        for r in range(1, group):
            x_copy(r).start()

    @pl.when(inner)
    def _():
        vrim_copy().wait_recv()
        ext_v[0:RIM_V] = vrim_in[...].astype(f32)

    @pl.when(jnp.logical_not(inner))
    def _():
        ext_v[0:RIM_V] = jnp.zeros((RIM_V, wide), f32)

    ext_v[RIM_V:] = values[...].astype(f32)
    running = conv_v[0:1] * ext_v[RIM_V:]
    for j in range(1, CONV):
        running = running + conv_v[j : j + 1] * ext_v[RIM_V - j : RIM_V - j + positions]
    conv_b[...] = running.astype(bf16)

    for r in range(1, n_fsdp):
        src = lax.rem(fsdp + r, n_fsdp)
        copy(part_in.at[src], part_in.at[src], part_ss.at[r], part_rs.at[src], (ctx, src, batch)).wait_recv()
    part_in[fsdp] = part_t[fsdp]
    raw = part_in[0]
    for s in range(1, n_fsdp):
        raw = raw + part_in[s]
    raw = raw.astype(bf16).astype(f32)

    @pl.when(inner)
    def _():
        for s in range(n_fsdp):
            copy(rim_in.at[s], rim_in.at[s], rim_ss.at[s], rim_rs.at[s], (ctx - 1, s, batch)).wait_recv()
        rows = rim_in[0]
        for s in range(1, n_fsdp):
            rows = rows + rim_in[s]
        rows = rows.astype(bf16).astype(f32)
        block = jnp.concatenate([jnp.zeros((positions - RIM, rows.shape[1]), f32), rows], axis=0)
        rim_t[...] = block.T

    @pl.when(jnp.logical_not(inner))
    def _():
        rim_t[...] = jnp.zeros(rim_t.shape, f32)

    before = rim_t[pl.ds(pl.multiple_of(fsdp * width, width), width), :]
    lane = lax.broadcasted_iota(jnp.int32, (width, positions), 1)
    taps = [column_of(conv_qk[j : j + 1]) for j in range(CONV)]
    running = taps[0] * raw
    for j in range(1, CONV):
        moved = jnp.where(lane < j, pltpu.roll(before, j, 1), pltpu.roll(raw, j, 1))
        running = running + taps[j] * moved
    qk_t = running.astype(bf16).astype(f32)
    qk = qk_t.T.astype(bf16)

    q_t = [qk_t[h * 2 * F : h * 2 * F + F] for h in range(heads)]
    k_t = [qk_t[h * 2 * F + F : (h + 1) * 2 * F] for h in range(heads)]
    fk_t = [features(k) for k in k_t]
    for h in range(heads):
        value = conv_b[:, h * E : (h + 1) * E]
        state_out[h] = dot(fk_t[h].astype(bf16), value).astype(bf16)

    def state_copy(r):
        return copy(state_out, state_in.at[ctx], state_ss.at[r], state_rs.at[ctx], (ctx + r, fsdp, batch))

    for r in range(1, n_ctx):
        @pl.when(ctx + r < n_ctx)
        def _():
            state_copy(r).start()

    fq_t = [features(q) for q in q_t]
    fq = [x.T.astype(bf16) for x in fq_t]
    fk = [x.T.astype(bf16) for x in fk_t]
    at_row = lax.broadcasted_iota(jnp.int32, (positions, positions), 0)
    at_col = lax.broadcasted_iota(jnp.int32, (positions, positions), 1)
    scores_t, kernels_t, local = [], [], []
    for h in range(heads):
        q, k = qk[:, h * 2 * F : h * 2 * F + F], qk[:, h * 2 * F + F : (h + 1) * 2 * F]
        score = dot(q, k_t[h].astype(bf16)) * F ** (-0.5)
        kernel = jnp.where(at_col <= at_row, 1.0 + score + 0.5 * score * score, 0.0).astype(bf16)
        local.append(dot(kernel, conv_b[:, h * E : (h + 1) * E]))
        score_t = dot(k, q_t[h].astype(bf16)) * F ** (-0.5)
        scores_t.append(score_t)
        kernels_t.append(
            jnp.where(at_row <= at_col, 1.0 + score_t + 0.5 * score_t * score_t, 0.0).astype(bf16)
        )

    prior[...] = jnp.zeros(prior.shape, f32)
    for s in range(n_ctx - 1):
        @pl.when(s < ctx)
        def _():
            copy(state_in.at[s], state_in.at[s], state_ss.at[s], state_rs.at[s], (s, fsdp, batch)).wait_recv()
            prior[...] += state_in[s].astype(f32)
    prior_b = [prior[h].astype(bf16) for h in range(heads)]
    for h in range(heads):
        lanes = slice(h * E, (h + 1) * E)
        mixed = local[h] + dot(fq[h], prior_b[h])
        inv = lax.rsqrt(jnp.mean(mixed * mixed, axis=-1, keepdims=True) + eps_norm)
        normed = mixed * inv
        attended[:, lanes] = normed.astype(bf16)
        g = d_attn[:, lanes].astype(f32)
        d_mixed = (inv * (g - normed * jnp.mean(g * normed, axis=-1, keepdims=True))).astype(bf16)
        mixed_b[:, lanes] = d_mixed
        grad_out[h] = dot(fq_t[h].astype(bf16), d_mixed).astype(bf16)

    def grad_copy(r):
        return copy(grad_out, grad_in.at[ctx], grad_ss.at[r], grad_rs.at[ctx], (ctx - r, fsdp, batch))

    for r in range(1, n_ctx):
        @pl.when(ctx - r >= 0)
        def _():
            grad_copy(r).start()

    d_q, d_k, d_v = [], [], []
    for h in range(heads):
        lanes = slice(h * E, (h + 1) * E)
        d_mixed, value = mixed_b[:, lanes], conv_b[:, lanes]
        d_kernel_t = dot_nt(value, d_mixed)
        d_score_t = jnp.where(
            at_row <= at_col, d_kernel_t * (1.0 + scores_t[h]), 0.0
        ) * F ** (-0.5)
        d_score_t = d_score_t.astype(bf16)
        d_q.append(
            dot(k_t[h].astype(bf16), d_score_t) + features_back(q_t[h], dot_nt(prior_b[h], d_mixed))
        )
        d_k.append(dot_nt(q_t[h].astype(bf16), d_score_t))
        d_v.append(dot(kernels_t[h], d_mixed))

    later[...] = jnp.zeros(later.shape, f32)
    for s in range(1, n_ctx):
        @pl.when(s > ctx)
        def _():
            copy(grad_in.at[s], grad_in.at[s], grad_ss.at[s], grad_rs.at[s], (s, fsdp, batch)).wait_recv()
            later[...] += grad_in[s].astype(f32)
    rows = []
    for h in range(heads):
        lanes = slice(h * E, (h + 1) * E)
        later_b = later[h].astype(bf16)
        back = features_back(k_t[h], dot_nt(later_b, conv_b[:, lanes]))
        rows += [d_q[h], d_k[h] + back]
        dv_ext[0:positions, lanes] = d_v[h] + dot(fk[h], later_b)
    d_qk_t = jnp.concatenate(rows, axis=0)
    dqk_out[...] = d_qk_t

    def dv_copy():
        return copy(
            dv_ext.at[pl.ds(0, RIM)], dv_ext.at[pl.ds(positions, RIM)], dv_ss, dv_rs, (ctx - 1, fsdp, batch)
        )

    def dqk_copy():
        return copy(dqk_out, dqk_in, dqk_ss, dqk_rs, (ctx - 1, fsdp, batch))

    @pl.when(inner)
    def _():
        dqk_copy().start()
        dv_copy().start()

    @pl.when(outer)
    def _():
        dqk_copy().wait_recv()

    @pl.when(jnp.logical_not(outer))
    def _():
        dqk_in[...] = jnp.zeros(dqk_in.shape, f32)
        dv_ext[positions:] = jnp.zeros((RIM, wide), f32)

    after = dqk_in[...]
    running = taps[0] * d_qk_t
    for j in range(1, CONV):
        moved = jnp.where(
            lane >= positions - j, pltpu.roll(after, positions - j, 1), pltpu.roll(d_qk_t, positions - j, 1)
        )
        running = running + taps[j] * moved
    d_pre = running.astype(bf16)

    def dq_copy(r):
        peer = lax.rem(me + r, group)
        return copy(
            dq_all.at[me], dq_all.at[me], dq_ss.at[r], dq_rs.at[me],
            (peer // n_batch, fsdp, lax.rem(peer, n_batch)),
        )

    if gather:
        dq_all[me] = d_pre
        for r in range(1, group):
            dq_copy(r).start()
    else:
        grad_w[...] = d_pre

    @pl.when(outer)
    def _():
        dv_copy().wait_recv()

    running = conv_v[0:1] * dv_ext[0:positions]
    for j in range(1, CONV):
        running = running + conv_v[j : j + 1] * dv_ext[j : j + positions]
    grad_v[...] = running.astype(bf16)

    if gather:
        total = dot(d_pre, tokens[:, pl.ds(pl.multiple_of(me * cols, cols), cols)])
        for r in range(1, group):
            src = lax.rem(me + r, group)
            to = (src // n_batch, fsdp, lax.rem(src, n_batch))
            copy(x_in.at[src], x_in.at[src], x_ss.at[r], x_rs.at[src], to).wait_recv()
            copy(dq_all.at[src], dq_all.at[src], dq_ss.at[r], dq_rs.at[src], to).wait_recv()
            total = total + dot(dq_all[src], x_in[src])
        grad_w[...] = total * float(positions * group) ** (-0.5)
        for r in range(1, group):
            x_copy(r).wait_send()
            dq_copy(r).wait_send()

    for r in range(1, n_fsdp):
        part_copy(r).wait_send()

    @pl.when(outer)
    def _():
        for r in range(n_fsdp):
            rim_copy(r).wait_send()
        vrim_copy().wait_send()

    @pl.when(inner)
    def _():
        dqk_copy().wait_send()
        dv_copy().wait_send()

    for r in range(1, n_ctx):
        @pl.when(ctx + r < n_ctx)
        def _():
            state_copy(r).wait_send()

        @pl.when(ctx - r >= 0)
        def _():
            grad_copy(r).wait_send()


def shards(dims, inputs, values, w_qk, conv_qk, conv_v, d_attn):
    n_ctx, n_fsdp, n_batch = dims
    tokens = inputs[0]
    positions, model = tokens.shape
    wide = values.shape[2]
    width = conv_qk.shape[1]
    heads = width // (2 * F)
    group = n_ctx * n_batch
    cols = model // group
    gather = cols % 128 == 0
    last = (width, cols) if gather else (width, positions)
    slots = group if gather else 1
    dma = pltpu.SemaphoreType.DMA
    state = (heads, PACKED, E)
    vmem = pl.BlockSpec(memory_space=pltpu.VMEM)
    scratch = [
        pltpu.VMEM((n_fsdp, width, positions), f32),
        pltpu.VMEM((n_fsdp, width, positions), f32),
        pltpu.VMEM((RIM, w_qk.shape[1]), f32),
        pltpu.VMEM((n_fsdp, RIM, w_qk.shape[1]), f32),
        pltpu.VMEM((w_qk.shape[1], positions), f32),
        pltpu.VMEM((RIM_V, wide), bf16),
        pltpu.VMEM((RIM_V + positions, wide), f32),
        pltpu.VMEM((positions, wide), bf16),
        pltpu.VMEM(state, bf16),
        pltpu.VMEM((n_ctx,) + state, bf16),
        pltpu.VMEM(state, f32),
        pltpu.VMEM(state, bf16),
        pltpu.VMEM((n_ctx,) + state, bf16),
        pltpu.VMEM(state, f32),
        pltpu.VMEM((positions, wide), bf16),
        pltpu.VMEM((positions + RIM, wide), f32),
        pltpu.VMEM((width, positions), f32),
        pltpu.VMEM((width, positions), f32),
        pltpu.VMEM((slots, positions, cols if gather else 128), bf16),
        pltpu.VMEM((slots, width, positions), bf16),
        dma((n_fsdp,)), dma((n_fsdp,)), dma((n_fsdp,)), dma((n_fsdp,)), dma, dma,
        dma((n_ctx,)), dma((n_ctx,)), dma((n_ctx,)), dma((n_ctx,)), dma, dma, dma, dma,
        dma((slots,)), dma((slots,)), dma((slots,)), dma((slots,)),
    ]
    attended, grad_v, tail = pl.pallas_call(
        functools.partial(body, (n_ctx, n_fsdp, n_batch, gather)),
        out_shape=(
            jax.ShapeDtypeStruct((positions, wide), bf16),
            jax.ShapeDtypeStruct((positions, wide), bf16),
            jax.ShapeDtypeStruct(last, f32 if gather else bf16),
        ),
        in_specs=[vmem] * 6,
        out_specs=(vmem,) * 3,
        scratch_shapes=scratch,
        compiler_params=pltpu.CompilerParams(
            collective_id=0, has_side_effects=True, vmem_limit_bytes=40 * 2**20
        ),
    )(tokens, values[0], w_qk, conv_qk, conv_v, d_attn[0])
    if gather:
        grad_w = tail.T
    else:
        grad_w = lax.psum_scatter(
            dot(tail, tokens).T, ("ctx", "batch"), scatter_dimension=0, tiled=True
        ) * float(positions * group) ** (-0.5)
    return (attended[None], grad_v[None], grad_w)


def solution(mesh):
    in_specs = (
        P("batch", "ctx", None),
        P("batch", "ctx", "fsdp"),
        P("fsdp", None),
        P(None, "fsdp"),
        P(None, "fsdp"),
        P("batch", "ctx", "fsdp"),
    )
    out_specs = (P("batch", "ctx", "fsdp"), P("batch", "ctx", "fsdp"), P(("ctx", "batch"), "fsdp"))
    dims = (mesh.shape["ctx"], mesh.shape["fsdp"], mesh.shape["batch"])
    return jax.shard_map(
        functools.partial(shards, dims), mesh=mesh, in_specs=in_specs, out_specs=out_specs, check_vma=False
    )
```

```python
import functools

import jax
import jax.numpy as jnp
from jax import lax
from jax.experimental import pallas as pl
from jax.experimental.pallas import tpu as pltpu
from jax.sharding import PartitionSpec as P

F = 16
E = 256
CONV = 3
PACKED = 8 * F + F // 2 + 8 + F
RIM_V = 16
RIM = 8

eps_norm = 1e-05
MESH = pl.DeviceIdType.MESH
bf16, f32 = jnp.bfloat16, jnp.float32


def dot(a, b):
    return jnp.dot(a, b, preferred_element_type=f32)


def dot_nt(a, b):
    return lax.dot_general(a, b, (((1,), (1,)), ((), ())), preferred_element_type=f32)


def turned(rows, by):
    if by == 0:
        return rows
    return jnp.concatenate([rows[by:], rows[:by]], axis=0)


def features(vec):
    positions = vec.shape[1]
    rows = [vec * vec * (2.0 * F) ** (-0.5)]
    scaled = vec * F ** (-0.5)
    for by in range(1, F // 2):
        rows.append(scaled * turned(vec, by))
    rows.append(scaled[: F // 2] * vec[F // 2 :])
    first = lax.broadcasted_iota(jnp.int32, (8, positions), 0) == 0
    rows.append(jnp.where(first, 1.0, 0.0).astype(f32))
    rows.append(vec * F ** (-0.25))
    return jnp.concatenate(rows, axis=0)


def features_back(vec, up):
    half = F // 2
    total = vec * up[:F] * (2.0 * (2.0 * F) ** (-0.5))
    total = total + up[8 * F + half + 8 :] * F ** (-0.25)
    pairs = jnp.zeros_like(vec)
    for by in range(1, half):
        part = up[by * F : (by + 1) * F]
        pairs = pairs + turned(vec, by) * part + turned(vec * part, F - by)
    part = up[half * F : half * F + half]
    pairs = pairs + jnp.concatenate([vec[half:] * part, vec[:half] * part], axis=0)
    return total + pairs * F ** (-0.5)


def column_of(row):
    n = row.shape[1]
    same = lax.broadcasted_iota(jnp.int32, (n, n), 0) == lax.broadcasted_iota(jnp.int32, (n, n), 1)
    return jnp.sum(jnp.where(same, row, 0.0), axis=1, keepdims=True)


def body(
    dims, tokens_h, values_h, weights_h, conv_qk_h, conv_v_h, d_attn_h,
    attended, grad_v, grad_w,
    tokens, values, weights, conv_qk, conv_v, d_attn,
    part_f, part_t, part_in, rim_out, rim_in, rim_t, vrim_in, ext_v, conv_b,
    state_out, state_in, prior, grad_out, grad_in, later, mixed_b,
    dv_ext, dqk_out, dqk_in, x_in, dq_all,
    part_ss, part_rs, rim_ss, rim_rs, vrim_ss, vrim_rs, state_ss, state_rs,
    grad_ss, grad_rs, dv_ss, dv_rs, dqk_ss, dqk_rs, x_ss, x_rs, dq_ss, dq_rs,
    load_s, pass_s, back_s,
):
    n_ctx, n_fsdp, n_batch, gather = dims
    ctx, fsdp, batch = lax.axis_index("ctx"), lax.axis_index("fsdp"), lax.axis_index("batch")
    positions = tokens.shape[0]
    depth = weights.shape[0]
    width = conv_qk.shape[1]
    heads = width // (2 * F)
    wide = values.shape[1]
    group = n_ctx * n_batch
    me = ctx * n_batch + batch
    inner, outer = ctx > 0, ctx < n_ctx - 1

    def copy(src, dst, ss, rs, to):
        return pltpu.make_async_remote_copy(
            src_ref=src, dst_ref=dst, send_sem=ss, recv_sem=rs, device_id=to, device_id_type=MESH
        )

    bar = pltpu.get_barrier_semaphore()

    def greet(to):
        pl.semaphore_signal(bar, inc=1, device_id=to, device_id_type=MESH)

    for r in range(1, n_fsdp):
        greet((ctx, lax.rem(fsdp + r, n_fsdp), batch))
    if gather:
        for r in range(1, group):
            peer = lax.rem(me + r, group)
            greet((peer // n_batch, fsdp, lax.rem(peer, n_batch)))
        count = group - 1 + n_fsdp - 1
        same = range(1, n_fsdp)
    else:
        for r in range(1, n_ctx):
            greet((lax.rem(ctx + r, n_ctx), fsdp, batch))
        count = n_ctx - 1 + n_fsdp - 1
        same = range(1, n_fsdp)

    @pl.when(inner)
    def _():
        for r in same:
            greet((ctx - 1, lax.rem(fsdp + r, n_fsdp), batch))

    @pl.when(outer)
    def _():
        for r in same:
            greet((ctx + 1, lax.rem(fsdp + r, n_fsdp), batch))

    loads = [
        pltpu.make_async_copy(src, dst, load_s.at[i])
        for i, (src, dst) in enumerate(
            [
                (weights_h, weights), (tokens_h, tokens), (values_h, values),
                (conv_v_h, conv_v), (conv_qk_h, conv_qk), (d_attn_h, d_attn),
            ]
        )
    ]
    for load in loads:
        load.start()
    loads[0].wait()
    loads[1].wait()

    columns = pl.ds(pl.multiple_of(fsdp * depth, depth), depth)
    part = dot(tokens[:, columns], weights[...])
    part_f[...] = part.T.reshape(part_f.shape)
    part_t[...] = part_f[...].astype(bf16)
    rim_out[...] = part[positions - RIM :]
    pl.semaphore_wait(
        bar, count + jnp.where(inner, n_fsdp - 1, 0) + jnp.where(outer, n_fsdp - 1, 0)
    )

    for load in loads[2:]:
        load.wait()

    def part_copy(r):
        peer = lax.rem(fsdp + r, n_fsdp)
        return copy(part_t.at[peer], part_in.at[fsdp], part_ss.at[r], part_rs.at[fsdp], (ctx, peer, batch))

    def rim_copy(r):
        peer = lax.rem(fsdp + r, n_fsdp)
        return copy(rim_out, rim_in.at[fsdp], rim_ss.at[r], rim_rs.at[fsdp], (ctx + 1, peer, batch))

    def vrim_copy():
        return copy(values.at[pl.ds(positions - RIM_V, RIM_V)], vrim_in, vrim_ss, vrim_rs, (ctx + 1, fsdp, batch))

    for r in range(1, n_fsdp):
        part_copy(r).start()

    @pl.when(outer)
    def _():
        for r in range(n_fsdp):
            rim_copy(r).start()
        vrim_copy().start()

    cols = tokens.shape[1] // group

    def x_copy(r):
        peer = lax.rem(me + r, group)
        return copy(
            tokens.at[:, pl.ds(pl.multiple_of(peer * cols, cols), cols)],
            x_in.at[me], x_ss.at[r], x_rs.at[me],
            (peer // n_batch, fsdp, lax.rem(peer, n_batch)),
        )

    pair = 2 if n_ctx % 2 == 0 else 1
    chip, core = ctx // pair, lax.rem(ctx, pair)
    mate = chip * pair + (pair - 1 - core)
    late = ctx < n_ctx // 2

    def x_start(first):
        for r in range(1, group):
            far = lax.rem(me + r, group) // (n_batch * pair) != chip
            held = jnp.logical_and(far, late)

            @pl.when(jnp.logical_not(held) if first else held)
            def _():
                x_copy(r).start()

    if gather:
        x_start(True)

    @pl.when(inner)
    def _():
        vrim_copy().wait_recv()
        ext_v[0:RIM_V] = vrim_in[...].astype(f32)

    @pl.when(jnp.logical_not(inner))
    def _():
        ext_v[0:RIM_V] = jnp.zeros((RIM_V, wide), f32)

    ext_v[RIM_V:] = values[...].astype(f32)
    running = conv_v[0:1] * ext_v[RIM_V:]
    for j in range(1, CONV):
        running = running + conv_v[j : j + 1] * ext_v[RIM_V - j : RIM_V - j + positions]
    conv_b[...] = running.astype(bf16)

    for r in range(1, n_fsdp):
        src = lax.rem(fsdp + r, n_fsdp)
        copy(part_in.at[src], part_in.at[src], part_ss.at[r], part_rs.at[src], (ctx, src, batch)).wait_recv()
    raw = part_f[fsdp]
    for r in range(1, n_fsdp):
        raw = raw + part_in[lax.rem(fsdp + r, n_fsdp)].astype(f32)
    raw = raw.astype(bf16).astype(f32)

    @pl.when(inner)
    def _():
        for s in range(n_fsdp):
            copy(rim_in.at[s], rim_in.at[s], rim_ss.at[s], rim_rs.at[s], (ctx - 1, s, batch)).wait_recv()
        rows = rim_in[0]
        for s in range(1, n_fsdp):
            rows = rows + rim_in[s]
        rows = rows.astype(bf16).astype(f32)
        block = jnp.concatenate([jnp.zeros((positions - RIM, rows.shape[1]), f32), rows], axis=0)
        rim_t[...] = block.T

    @pl.when(jnp.logical_not(inner))
    def _():
        rim_t[...] = jnp.zeros(rim_t.shape, f32)

    before = rim_t[pl.ds(pl.multiple_of(fsdp * width, width), width), :]
    lane = lax.broadcasted_iota(jnp.int32, (width, positions), 1)
    taps = [column_of(conv_qk[j : j + 1]) for j in range(CONV)]
    running = taps[0] * raw
    for j in range(1, CONV):
        moved = jnp.where(lane < j, pltpu.roll(before, j, 1), pltpu.roll(raw, j, 1))
        running = running + taps[j] * moved
    qk_t = running.astype(bf16).astype(f32)
    qk = qk_t.T.astype(bf16)

    q_t = [qk_t[h * 2 * F : h * 2 * F + F] for h in range(heads)]
    k_t = [qk_t[h * 2 * F + F : (h + 1) * 2 * F] for h in range(heads)]
    fk_t = [features(k) for k in k_t]

    def sent(out, into, ss, rs, h, to, i):
        return copy(out.at[h], into.at[ctx, h], ss.at[i, h], rs.at[ctx, h], (to, fsdp, batch))

    def send(out, into, ss, rs, h, sign, done):
        def act(c):
            c.wait_send() if done else c.start()

        if pair == 2:
            @pl.when(core == (0 if sign > 0 else 1))
            def _():
                act(sent(out, into, ss, rs, h, mate, 0))

        for i in range(1, n_ctx // pair):
            to = ctx + sign * pair * i

            @pl.when(jnp.logical_and(to >= 0, to < n_ctx))
            def _():
                act(sent(out, into, ss, rs, h, to, i))

    def passed(into, rs, ps, s, h):
        return copy(into.at[s, h], into.at[s, h], ps.at[s, h], rs.at[s, h], (mate, fsdp, batch))

    def relays(s, sign):
        if pair == 1:
            return s < 0
        there = s // pair < chip if sign > 0 else s // pair > chip
        return jnp.logical_and(there, core == s % pair)

    def receive(into, rs, ps, total, h, sign):
        for s in range(n_ctx):
            if pair == 2:
                @pl.when(relays(s, sign))
                def _():
                    passed(into, rs, ps, s, h).wait_recv()
                    passed(into, rs, ps, s, h).start()
        total[h] = jnp.zeros(total.shape[1:], f32)
        for s in range(n_ctx):
            wanted = s < ctx if sign > 0 else s > ctx
            plain = jnp.logical_and(wanted, jnp.logical_not(relays(s, sign))) if pair == 2 else wanted

            @pl.when(plain)
            def _():
                passed(into, rs, ps, s, h).wait_recv()

            @pl.when(wanted)
            def _():
                total[h] += into[s, h].astype(f32)

    def finish(out, into, ss, rs, ps, sign):
        for h in range(heads):
            send(out, into, ss, rs, h, sign, True)
            if pair == 2:
                for s in range(n_ctx):
                    @pl.when(relays(s, sign))
                    def _():
                        passed(into, rs, ps, s, h).wait_send()

    for h in range(heads):
        state_out[h] = dot(fk_t[h].astype(bf16), conv_b[:, h * E : (h + 1) * E]).astype(bf16)
        send(state_out, state_in, state_ss, state_rs, h, 1, False)
    if gather:
        x_start(False)

    fq_t = [features(q) for q in q_t]
    fq = [x.T.astype(bf16) for x in fq_t]
    fk = [x.T.astype(bf16) for x in fk_t]
    at_row = lax.broadcasted_iota(jnp.int32, (positions, positions), 0)
    at_col = lax.broadcasted_iota(jnp.int32, (positions, positions), 1)
    scores_t, kernels_t, local = [], [], []
    for h in range(heads):
        q, k = qk[:, h * 2 * F : h * 2 * F + F], qk[:, h * 2 * F + F : (h + 1) * 2 * F]
        score = dot(q, k_t[h].astype(bf16)) * F ** (-0.5)
        kernel = jnp.where(at_col <= at_row, 1.0 + score + 0.5 * score * score, 0.0).astype(bf16)
        local.append(dot(kernel, conv_b[:, h * E : (h + 1) * E]))
        score_t = dot(k, q_t[h].astype(bf16)) * F ** (-0.5)
        scores_t.append(score_t)
        kernels_t.append(
            jnp.where(at_row <= at_col, 1.0 + score_t + 0.5 * score_t * score_t, 0.0).astype(bf16)
        )

    prior_b = []
    for h in range(heads):
        lanes = slice(h * E, (h + 1) * E)
        receive(state_in, state_rs, pass_s, prior, h, 1)
        prior_b.append(prior[h].astype(bf16))
        mixed = local[h] + dot(fq[h], prior_b[h])
        inv = lax.rsqrt(jnp.mean(mixed * mixed, axis=-1, keepdims=True) + eps_norm)
        normed = mixed * inv
        attended[:, lanes] = normed.astype(bf16)
        g = d_attn[:, lanes].astype(f32)
        d_mixed = (inv * (g - normed * jnp.mean(g * normed, axis=-1, keepdims=True))).astype(bf16)
        mixed_b[:, lanes] = d_mixed
        grad_out[h] = dot(fq_t[h].astype(bf16), d_mixed).astype(bf16)
        send(grad_out, grad_in, grad_ss, grad_rs, h, -1, False)

    d_q, d_k, d_v = [], [], []
    for h in range(heads):
        lanes = slice(h * E, (h + 1) * E)
        d_mixed, value = mixed_b[:, lanes], conv_b[:, lanes]
        d_kernel_t = dot_nt(value, d_mixed)
        d_score_t = jnp.where(
            at_row <= at_col, d_kernel_t * (1.0 + scores_t[h]), 0.0
        ) * F ** (-0.5)
        d_score_t = d_score_t.astype(bf16)
        d_q.append(
            dot(k_t[h].astype(bf16), d_score_t) + features_back(q_t[h], dot_nt(prior_b[h], d_mixed))
        )
        d_k.append(dot_nt(q_t[h].astype(bf16), d_score_t))
        d_v.append(dot(kernels_t[h], d_mixed))

    rows, later_b = [], []
    for h in range(heads):
        receive(grad_in, grad_rs, back_s, later, h, -1)
        later_b.append(later[h].astype(bf16))
        back = features_back(k_t[h], dot_nt(later_b[h], conv_b[:, h * E : (h + 1) * E]))
        rows += [d_q[h], d_k[h] + back]
    d_qk_t = jnp.concatenate(rows, axis=0)
    dqk_out[...] = d_qk_t

    def dv_copy():
        return copy(
            dv_ext.at[pl.ds(0, RIM)], dv_ext.at[pl.ds(positions, RIM)], dv_ss, dv_rs, (ctx - 1, fsdp, batch)
        )

    def dqk_copy():
        return copy(dqk_out, dqk_in, dqk_ss, dqk_rs, (ctx - 1, fsdp, batch))

    @pl.when(inner)
    def _():
        dqk_copy().start()

    for h in range(heads):
        dv_ext[0:positions, h * E : (h + 1) * E] = d_v[h] + dot(fk[h], later_b[h])

    @pl.when(inner)
    def _():
        dv_copy().start()

    @pl.when(outer)
    def _():
        dqk_copy().wait_recv()

    @pl.when(jnp.logical_not(outer))
    def _():
        dqk_in[...] = jnp.zeros(dqk_in.shape, f32)
        dv_ext[positions:] = jnp.zeros((RIM, wide), f32)

    after = dqk_in[...]
    running = taps[0] * d_qk_t
    for j in range(1, CONV):
        moved = jnp.where(
            lane >= positions - j, pltpu.roll(after, positions - j, 1), pltpu.roll(d_qk_t, positions - j, 1)
        )
        running = running + taps[j] * moved
    d_pre = running.astype(bf16)

    def dq_copy(r):
        peer = lax.rem(me + r, group)
        return copy(
            dq_all.at[me], dq_all.at[me], dq_ss.at[r], dq_rs.at[me],
            (peer // n_batch, fsdp, lax.rem(peer, n_batch)),
        )

    if gather:
        dq_all[me] = d_pre
        for r in range(1, group):
            dq_copy(r).start()
    else:
        grad_w[...] = d_pre

    @pl.when(outer)
    def _():
        dv_copy().wait_recv()

    running = conv_v[0:1] * dv_ext[0:positions]
    for j in range(1, CONV):
        running = running + conv_v[j : j + 1] * dv_ext[j : j + positions]
    grad_v[...] = running.astype(bf16)

    if gather:
        total = dot(d_pre, tokens[:, pl.ds(pl.multiple_of(me * cols, cols), cols)])
        for r in range(1, group):
            src = lax.rem(me + r, group)
            to = (src // n_batch, fsdp, lax.rem(src, n_batch))
            copy(x_in.at[src], x_in.at[src], x_ss.at[r], x_rs.at[src], to).wait_recv()
            copy(dq_all.at[src], dq_all.at[src], dq_ss.at[r], dq_rs.at[src], to).wait_recv()
            total = total + dot(dq_all[src], x_in[src])
        grad_w[...] = total * float(positions * group) ** (-0.5)
        for r in range(1, group):
            x_copy(r).wait_send()
            dq_copy(r).wait_send()

    for r in range(1, n_fsdp):
        part_copy(r).wait_send()

    @pl.when(outer)
    def _():
        for r in range(n_fsdp):
            rim_copy(r).wait_send()
        vrim_copy().wait_send()

    @pl.when(inner)
    def _():
        dqk_copy().wait_send()
        dv_copy().wait_send()

    finish(state_out, state_in, state_ss, state_rs, pass_s, 1)
    finish(grad_out, grad_in, grad_ss, grad_rs, back_s, -1)


def write(*refs):
    *blocks, sems = refs
    n = len(blocks) // 2
    copies = [pltpu.make_async_copy(blocks[i], blocks[n + i], sems.at[i]) for i in range(n)]
    for c in copies:
        c.start()
    for c in copies:
        c.wait()


def shards(dims, inputs, values, w_qk, conv_qk, conv_v, d_attn):
    n_ctx, n_fsdp, n_batch = dims
    tokens = inputs[0]
    positions, model = tokens.shape
    wide = values.shape[2]
    width = conv_qk.shape[1]
    heads = width // (2 * F)
    group = n_ctx * n_batch
    cols = model // group
    gather = cols % 128 == 0
    last = (width, cols) if gather else (width, positions)
    slots = group if gather else 1
    dma = pltpu.SemaphoreType.DMA
    state = (heads, PACKED, E)
    vmem = pl.BlockSpec(memory_space=pltpu.VMEM)
    hbm = pl.BlockSpec(memory_space=pl.ANY)
    scratch = [
        pltpu.VMEM(tokens.shape, bf16),
        pltpu.VMEM((positions, wide), bf16),
        pltpu.VMEM(w_qk.shape, bf16),
        pltpu.VMEM(conv_qk.shape, f32),
        pltpu.VMEM(conv_v.shape, f32),
        pltpu.VMEM((positions, wide), bf16),
        pltpu.VMEM((n_fsdp, width, positions), f32),
        pltpu.VMEM((n_fsdp, width, positions), bf16),
        pltpu.VMEM((n_fsdp, width, positions), bf16),
        pltpu.VMEM((RIM, w_qk.shape[1]), f32),
        pltpu.VMEM((n_fsdp, RIM, w_qk.shape[1]), f32),
        pltpu.VMEM((w_qk.shape[1], positions), f32),
        pltpu.VMEM((RIM_V, wide), bf16),
        pltpu.VMEM((RIM_V + positions, wide), f32),
        pltpu.VMEM((positions, wide), bf16),
        pltpu.VMEM(state, bf16),
        pltpu.VMEM((n_ctx,) + state, bf16),
        pltpu.VMEM(state, f32),
        pltpu.VMEM(state, bf16),
        pltpu.VMEM((n_ctx,) + state, bf16),
        pltpu.VMEM(state, f32),
        pltpu.VMEM((positions, wide), bf16),
        pltpu.VMEM((positions + RIM, wide), f32),
        pltpu.VMEM((width, positions), f32),
        pltpu.VMEM((width, positions), f32),
        pltpu.VMEM((slots, positions, cols if gather else 128), bf16),
        pltpu.VMEM((slots, width, positions), bf16),
        dma((n_fsdp,)), dma((n_fsdp,)), dma((n_fsdp,)), dma((n_fsdp,)), dma, dma,
        dma((n_ctx, heads)), dma((n_ctx, heads)), dma((n_ctx, heads)), dma((n_ctx, heads)),
        dma, dma, dma, dma,
        dma((slots,)), dma((slots,)), dma((slots,)), dma((slots,)),
        dma((6,)), dma((n_ctx, heads)), dma((n_ctx, heads)),
    ]
    attended, grad_v, tail = pl.pallas_call(
        functools.partial(body, (n_ctx, n_fsdp, n_batch, gather)),
        out_shape=(
            jax.ShapeDtypeStruct((positions, wide), bf16),
            jax.ShapeDtypeStruct((positions, wide), bf16),
            jax.ShapeDtypeStruct(last, f32 if gather else bf16),
        ),
        in_specs=[hbm] * 6,
        out_specs=(vmem,) * 3,
        scratch_shapes=scratch,
        compiler_params=pltpu.CompilerParams(
            collective_id=0, has_side_effects=True, vmem_limit_bytes=56 * 2**20
        ),
    )(tokens, values[0], w_qk, conv_qk, conv_v, d_attn[0])
    if gather:
        blocks = (attended, grad_v, tail)
        attended, grad_v, tail = pl.pallas_call(
            write,
            out_shape=tuple(jax.ShapeDtypeStruct(x.shape, x.dtype) for x in blocks),
            in_specs=[pl.BlockSpec(memory_space=pltpu.HBM)] * 3,
            out_specs=(pl.BlockSpec(memory_space=pltpu.HBM),) * 3,
            scratch_shapes=[dma((3,))],
        )(*blocks)
        grad_w = tail.T
    else:
        grad_w = lax.psum_scatter(
            dot(tail, tokens).T, ("ctx", "batch"), scatter_dimension=0, tiled=True
        ) * float(positions * group) ** (-0.5)
    return (attended[None], grad_v[None], grad_w)


def solution(mesh):
    in_specs = (
        P("batch", "ctx", None),
        P("batch", "ctx", "fsdp"),
        P("fsdp", None),
        P(None, "fsdp"),
        P(None, "fsdp"),
        P("batch", "ctx", "fsdp"),
    )
    out_specs = (P("batch", "ctx", "fsdp"), P("batch", "ctx", "fsdp"), P(("ctx", "batch"), "fsdp"))
    dims = (mesh.shape["ctx"], mesh.shape["fsdp"], mesh.shape["batch"])
    return jax.shard_map(
        functools.partial(shards, dims), mesh=mesh, in_specs=in_specs, out_specs=out_specs, check_vma=False
    )
```

```python
import functools

import jax
import jax.numpy as jnp
from jax import lax
from jax.experimental import pallas as pl
from jax.experimental.pallas import tpu as pltpu
from jax.sharding import PartitionSpec as P

F = 16
E = 256
CONV = 3
PACKED = 8 * F + F // 2 + 8 + F
RIM_V = 16
RIM = 8

eps_norm = 1e-05
MESH = pl.DeviceIdType.MESH
bf16, f32 = jnp.bfloat16, jnp.float32


def dot(a, b):
    return jnp.dot(a, b, preferred_element_type=f32)


def dot_nt(a, b):
    return lax.dot_general(a, b, (((1,), (1,)), ((), ())), preferred_element_type=f32)


def turned(rows, by):
    if by == 0:
        return rows
    return jnp.concatenate([rows[by:], rows[:by]], axis=0)


def features(vec):
    positions = vec.shape[1]
    rows = [vec * vec * (2.0 * F) ** (-0.5)]
    scaled = vec * F ** (-0.5)
    for by in range(1, F // 2):
        rows.append(scaled * turned(vec, by))
    rows.append(scaled[: F // 2] * vec[F // 2 :])
    first = lax.broadcasted_iota(jnp.int32, (8, positions), 0) == 0
    rows.append(jnp.where(first, 1.0, 0.0).astype(f32))
    rows.append(vec * F ** (-0.25))
    return jnp.concatenate(rows, axis=0)


def features_back(vec, up):
    half = F // 2
    total = vec * up[:F] * (2.0 * (2.0 * F) ** (-0.5))
    total = total + up[8 * F + half + 8 :] * F ** (-0.25)
    pairs = jnp.zeros_like(vec)
    for by in range(1, half):
        part = up[by * F : (by + 1) * F]
        pairs = pairs + turned(vec, by) * part + turned(vec * part, F - by)
    part = up[half * F : half * F + half]
    pairs = pairs + jnp.concatenate([vec[half:] * part, vec[:half] * part], axis=0)
    return total + pairs * F ** (-0.5)


def column_of(row):
    n = row.shape[1]
    same = lax.broadcasted_iota(jnp.int32, (n, n), 0) == lax.broadcasted_iota(jnp.int32, (n, n), 1)
    return jnp.sum(jnp.where(same, row, 0.0), axis=1, keepdims=True)


def body(
    dims, tokens_h, values_h, weights_h, conv_qk_h, conv_v_h, d_attn_h,
    attended, grad_v, grad_w,
    tokens, values, weights, conv_qk, conv_v, d_attn, own,
    part_f, part_t, part_in, rim_out, rim_in, rim_t, vrim_in, ext_v, conv_b,
    state_out, state_in, prior, grad_out, grad_in, later, mixed_b,
    dv_ext, dqk_out, dqk_in, x_in, dq_all,
    part_ss, part_rs, rim_ss, rim_rs, vrim_ss, vrim_rs, state_ss, state_rs,
    grad_ss, grad_rs, dv_ss, dv_rs, dqk_ss, dqk_rs, x_ss, x_rs, dq_ss, dq_rs,
    load_s, pass_s, back_s,
):
    n_ctx, n_fsdp, n_batch, gather = dims
    ctx, fsdp, batch = lax.axis_index("ctx"), lax.axis_index("fsdp"), lax.axis_index("batch")
    positions = tokens.shape[0]
    depth = weights.shape[0]
    width = conv_qk.shape[1]
    heads = width // (2 * F)
    wide = values.shape[1]
    group = n_ctx * n_batch
    me = ctx * n_batch + batch
    inner, outer = ctx > 0, ctx < n_ctx - 1

    def copy(src, dst, ss, rs, to):
        return pltpu.make_async_remote_copy(
            src_ref=src, dst_ref=dst, send_sem=ss, recv_sem=rs, device_id=to, device_id_type=MESH
        )

    bar = pltpu.get_barrier_semaphore()

    def greet(to):
        pl.semaphore_signal(bar, inc=1, device_id=to, device_id_type=MESH)

    for r in range(1, n_fsdp):
        greet((ctx, lax.rem(fsdp + r, n_fsdp), batch))
    if gather:
        for r in range(1, group):
            peer = lax.rem(me + r, group)
            greet((peer // n_batch, fsdp, lax.rem(peer, n_batch)))
        count = group - 1 + n_fsdp - 1
        same = range(1, n_fsdp)
    else:
        for r in range(1, n_ctx):
            greet((lax.rem(ctx + r, n_ctx), fsdp, batch))
        count = n_ctx - 1 + n_fsdp - 1
        same = range(1, n_fsdp)

    @pl.when(inner)
    def _():
        for r in same:
            greet((ctx - 1, lax.rem(fsdp + r, n_fsdp), batch))

    @pl.when(outer)
    def _():
        for r in same:
            greet((ctx + 1, lax.rem(fsdp + r, n_fsdp), batch))

    columns = pl.ds(pl.multiple_of(fsdp * depth, depth), depth)
    loads = [
        pltpu.make_async_copy(src, dst, load_s.at[i])
        for i, (src, dst) in enumerate(
            [
                (weights_h, weights), (tokens_h.at[:, columns], own), (values_h, values),
                (conv_v_h, conv_v), (conv_qk_h, conv_qk), (tokens_h, tokens), (d_attn_h, d_attn),
            ]
        )
    ]
    for load in loads:
        load.start()
    loads[0].wait()
    loads[1].wait()

    part = dot(own[...], weights[...])
    part_f[...] = part.T.reshape(part_f.shape)
    part_t[...] = part_f[...].astype(bf16)
    rim_out[...] = part[positions - RIM :]
    pl.semaphore_wait(
        bar, count + jnp.where(inner, n_fsdp - 1, 0) + jnp.where(outer, n_fsdp - 1, 0)
    )

    for load in loads[2:]:
        load.wait()

    def part_copy(r):
        peer = lax.rem(fsdp + r, n_fsdp)
        return copy(part_t.at[peer], part_in.at[fsdp], part_ss.at[r], part_rs.at[fsdp], (ctx, peer, batch))

    def rim_copy(r):
        peer = lax.rem(fsdp + r, n_fsdp)
        return copy(rim_out, rim_in.at[fsdp], rim_ss.at[r], rim_rs.at[fsdp], (ctx + 1, peer, batch))

    def vrim_copy():
        return copy(values.at[pl.ds(positions - RIM_V, RIM_V)], vrim_in, vrim_ss, vrim_rs, (ctx + 1, fsdp, batch))

    for r in range(1, n_fsdp):
        part_copy(r).start()

    @pl.when(outer)
    def _():
        for r in range(n_fsdp):
            rim_copy(r).start()
        vrim_copy().start()

    cols = tokens.shape[1] // group

    def x_copy(r):
        peer = lax.rem(me + r, group)
        return copy(
            tokens.at[:, pl.ds(pl.multiple_of(peer * cols, cols), cols)],
            x_in.at[me], x_ss.at[r], x_rs.at[me],
            (peer // n_batch, fsdp, lax.rem(peer, n_batch)),
        )

    pair = 2 if n_ctx % 2 == 0 else 1
    chip, core = ctx // pair, lax.rem(ctx, pair)
    mate = chip * pair + (pair - 1 - core)
    late = ctx < n_ctx // 2

    def x_start(first):
        for r in range(1, group):
            far = lax.rem(me + r, group) // (n_batch * pair) != chip
            held = jnp.logical_and(far, late)

            @pl.when(jnp.logical_not(held) if first else held)
            def _():
                x_copy(r).start()

    if gather:
        x_in[me] = tokens[:, pl.ds(pl.multiple_of(me * cols, cols), cols)]
        x_start(True)

    @pl.when(inner)
    def _():
        vrim_copy().wait_recv()
        ext_v[0:RIM_V] = vrim_in[...].astype(f32)

    @pl.when(jnp.logical_not(inner))
    def _():
        ext_v[0:RIM_V] = jnp.zeros((RIM_V, wide), f32)

    ext_v[RIM_V:] = values[...].astype(f32)
    running = conv_v[0:1] * ext_v[RIM_V:]
    for j in range(1, CONV):
        running = running + conv_v[j : j + 1] * ext_v[RIM_V - j : RIM_V - j + positions]
    conv_b[...] = running.astype(bf16)

    for r in range(1, n_fsdp):
        src = lax.rem(fsdp + r, n_fsdp)
        copy(part_in.at[src], part_in.at[src], part_ss.at[r], part_rs.at[src], (ctx, src, batch)).wait_recv()
    raw = part_f[fsdp]
    for r in range(1, n_fsdp):
        raw = raw + part_in[lax.rem(fsdp + r, n_fsdp)].astype(f32)
    raw = raw.astype(bf16).astype(f32)

    @pl.when(inner)
    def _():
        for s in range(n_fsdp):
            copy(rim_in.at[s], rim_in.at[s], rim_ss.at[s], rim_rs.at[s], (ctx - 1, s, batch)).wait_recv()
        rows = rim_in[0]
        for s in range(1, n_fsdp):
            rows = rows + rim_in[s]
        rows = rows.astype(bf16).astype(f32)
        block = jnp.concatenate([jnp.zeros((positions - RIM, rows.shape[1]), f32), rows], axis=0)
        rim_t[...] = block.T

    @pl.when(jnp.logical_not(inner))
    def _():
        rim_t[...] = jnp.zeros(rim_t.shape, f32)

    before = rim_t[pl.ds(pl.multiple_of(fsdp * width, width), width), :]
    lane = lax.broadcasted_iota(jnp.int32, (width, positions), 1)
    taps = [column_of(conv_qk[j : j + 1]) for j in range(CONV)]
    running = taps[0] * raw
    for j in range(1, CONV):
        moved = jnp.where(lane < j, pltpu.roll(before, j, 1), pltpu.roll(raw, j, 1))
        running = running + taps[j] * moved
    qk_t = running.astype(bf16).astype(f32)
    qk = qk_t.T.astype(bf16)

    q_t = [qk_t[h * 2 * F : h * 2 * F + F] for h in range(heads)]
    k_t = [qk_t[h * 2 * F + F : (h + 1) * 2 * F] for h in range(heads)]
    fk_t = [features(k) for k in k_t]

    def sent(out, into, ss, rs, h, to, i):
        return copy(out.at[h], into.at[ctx, h], ss.at[i, h], rs.at[ctx, h], (to, fsdp, batch))

    def send(out, into, ss, rs, h, sign, done):
        def act(c):
            c.wait_send() if done else c.start()

        if pair == 2:
            @pl.when(core == (0 if sign > 0 else 1))
            def _():
                act(sent(out, into, ss, rs, h, mate, 0))

        for i in range(1, n_ctx // pair):
            to = ctx + sign * pair * i

            @pl.when(jnp.logical_and(to >= 0, to < n_ctx))
            def _():
                act(sent(out, into, ss, rs, h, to, i))

    def passed(into, rs, ps, s, h):
        return copy(into.at[s, h], into.at[s, h], ps.at[s, h], rs.at[s, h], (mate, fsdp, batch))

    def relays(s, sign):
        if pair == 1:
            return s < 0
        there = s // pair < chip if sign > 0 else s // pair > chip
        return jnp.logical_and(there, core == s % pair)

    def receive(into, rs, ps, total, h, sign):
        for s in range(n_ctx):
            if pair == 2:
                @pl.when(relays(s, sign))
                def _():
                    passed(into, rs, ps, s, h).wait_recv()
                    passed(into, rs, ps, s, h).start()
        total[h] = jnp.zeros(total.shape[1:], f32)
        for s in range(n_ctx):
            wanted = s < ctx if sign > 0 else s > ctx
            plain = jnp.logical_and(wanted, jnp.logical_not(relays(s, sign))) if pair == 2 else wanted

            @pl.when(plain)
            def _():
                passed(into, rs, ps, s, h).wait_recv()

            @pl.when(wanted)
            def _():
                total[h] += into[s, h].astype(f32)

    def finish(out, into, ss, rs, ps, sign):
        for h in range(heads):
            send(out, into, ss, rs, h, sign, True)
            if pair == 2:
                for s in range(n_ctx):
                    @pl.when(relays(s, sign))
                    def _():
                        passed(into, rs, ps, s, h).wait_send()

    for h in range(heads):
        state_out[h] = dot(fk_t[h].astype(bf16), conv_b[:, h * E : (h + 1) * E]).astype(bf16)
        send(state_out, state_in, state_ss, state_rs, h, 1, False)
    fq_t = [features(q) for q in q_t]
    fq = [x.T.astype(bf16) for x in fq_t]
    fk = [x.T.astype(bf16) for x in fk_t]
    at_row = lax.broadcasted_iota(jnp.int32, (positions, positions), 0)
    at_col = lax.broadcasted_iota(jnp.int32, (positions, positions), 1)
    scores_t, kernels_t, local = [], [], []
    for h in range(heads):
        q, k = qk[:, h * 2 * F : h * 2 * F + F], qk[:, h * 2 * F + F : (h + 1) * 2 * F]
        score = dot(q, k_t[h].astype(bf16)) * F ** (-0.5)
        kernel = jnp.where(at_col <= at_row, 1.0 + score + 0.5 * score * score, 0.0).astype(bf16)
        local.append(dot(kernel, conv_b[:, h * E : (h + 1) * E]))
        score_t = dot(k, q_t[h].astype(bf16)) * F ** (-0.5)
        scores_t.append(score_t)
        kernels_t.append(
            jnp.where(at_row <= at_col, 1.0 + score_t + 0.5 * score_t * score_t, 0.0).astype(bf16)
        )

    if gather:
        x_start(False)

    prior_b = []
    for h in range(heads):
        lanes = slice(h * E, (h + 1) * E)
        receive(state_in, state_rs, pass_s, prior, h, 1)
        prior_b.append(prior[h].astype(bf16))
        mixed = local[h] + dot(fq[h], prior_b[h])
        inv = lax.rsqrt(jnp.mean(mixed * mixed, axis=-1, keepdims=True) + eps_norm)
        normed = mixed * inv
        attended[:, lanes] = normed.astype(bf16)
        g = d_attn[:, lanes].astype(f32)
        d_mixed = (inv * (g - normed * jnp.mean(g * normed, axis=-1, keepdims=True))).astype(bf16)
        mixed_b[:, lanes] = d_mixed
        grad_out[h] = dot(fq_t[h].astype(bf16), d_mixed).astype(bf16)
        send(grad_out, grad_in, grad_ss, grad_rs, h, -1, False)

    d_q, d_k, d_v = [], [], []
    for h in range(heads):
        lanes = slice(h * E, (h + 1) * E)
        d_mixed, value = mixed_b[:, lanes], conv_b[:, lanes]
        d_kernel_t = dot_nt(value, d_mixed)
        d_score_t = jnp.where(
            at_row <= at_col, d_kernel_t * (1.0 + scores_t[h]), 0.0
        ) * F ** (-0.5)
        d_score_t = d_score_t.astype(bf16)
        d_q.append(
            dot(k_t[h].astype(bf16), d_score_t) + features_back(q_t[h], dot_nt(prior_b[h], d_mixed))
        )
        d_k.append(dot_nt(q_t[h].astype(bf16), d_score_t))
        d_v.append(dot(kernels_t[h], d_mixed))

    rows, later_b = [], []
    for h in range(heads):
        receive(grad_in, grad_rs, back_s, later, h, -1)
        later_b.append(later[h].astype(bf16))
        back = features_back(k_t[h], dot_nt(later_b[h], conv_b[:, h * E : (h + 1) * E]))
        rows += [d_q[h], d_k[h] + back]
    d_qk_t = jnp.concatenate(rows, axis=0)

    def dq_copy(r):
        peer = lax.rem(me + r, group)
        return copy(
            dq_all.at[me], dq_all.at[me], dq_ss.at[r], dq_rs.at[me],
            (peer // n_batch, fsdp, lax.rem(peer, n_batch)),
        )

    def dqk_copy():
        return copy(dqk_out, dqk_in, dqk_ss, dqk_rs, (ctx - 1, fsdp, batch))

    if gather:
        dq_all[me] = d_qk_t.astype(bf16)
        for r in range(1, group):
            dq_copy(r).start()
    else:
        dqk_out[...] = d_qk_t

        @pl.when(inner)
        def _():
            dqk_copy().start()

    def dv_copy():
        return copy(
            dv_ext.at[pl.ds(0, RIM)], dv_ext.at[pl.ds(positions, RIM)], dv_ss, dv_rs, (ctx - 1, fsdp, batch)
        )

    for h in range(heads):
        dv_ext[0:positions, h * E : (h + 1) * E] = d_v[h] + dot(fk[h], later_b[h])

    @pl.when(inner)
    def _():
        dv_copy().start()

    def convolve_back(here, after):
        running = taps[0] * here
        for j in range(1, CONV):
            moved = pltpu.roll(here, positions - j, 1)
            rim = 0.0 if after is None else pltpu.roll(after, positions - j, 1)
            running = running + taps[j] * jnp.where(lane >= positions - j, rim, moved)
        return running.astype(bf16)

    if not gather:
        @pl.when(outer)
        def _():
            dqk_copy().wait_recv()

        @pl.when(jnp.logical_not(outer))
        def _():
            dqk_in[...] = jnp.zeros(dqk_in.shape, f32)

        grad_w[...] = convolve_back(d_qk_t, dqk_in[...])

    @pl.when(outer)
    def _():
        dv_copy().wait_recv()

    @pl.when(jnp.logical_not(outer))
    def _():
        dv_ext[positions:] = jnp.zeros((RIM, wide), f32)

    running = conv_v[0:1] * dv_ext[0:positions]
    for j in range(1, CONV):
        running = running + conv_v[j : j + 1] * dv_ext[j : j + positions]
    grad_v[...] = running.astype(bf16)

    if gather:
        for r in range(1, group):
            src = lax.rem(me + r, group)
            to = (src // n_batch, fsdp, lax.rem(src, n_batch))
            copy(x_in.at[src], x_in.at[src], x_ss.at[r], x_rs.at[src], to).wait_recv()
            copy(dq_all.at[src], dq_all.at[src], dq_ss.at[r], dq_rs.at[src], to).wait_recv()
        blocks = [dq_all[s].astype(f32) for s in range(group)]
        d_pre = [
            convolve_back(blocks[s], blocks[s + n_batch] if s + n_batch < group else None)
            for s in range(group)
        ]
        total = dot(jnp.concatenate(d_pre, axis=1), x_in[...].reshape(group * positions, cols))
        grad_w[...] = total * float(positions * group) ** (-0.5)
        for r in range(1, group):
            x_copy(r).wait_send()
            dq_copy(r).wait_send()

    for r in range(1, n_fsdp):
        part_copy(r).wait_send()

    @pl.when(outer)
    def _():
        for r in range(n_fsdp):
            rim_copy(r).wait_send()
        vrim_copy().wait_send()

    @pl.when(inner)
    def _():
        if not gather:
            dqk_copy().wait_send()
        dv_copy().wait_send()

    finish(state_out, state_in, state_ss, state_rs, pass_s, 1)
    finish(grad_out, grad_in, grad_ss, grad_rs, back_s, -1)


def shards(dims, inputs, values, w_qk, conv_qk, conv_v, d_attn):
    n_ctx, n_fsdp, n_batch = dims
    tokens = inputs[0]
    positions, model = tokens.shape
    wide = values.shape[2]
    width = conv_qk.shape[1]
    heads = width // (2 * F)
    group = n_ctx * n_batch
    cols = model // group
    gather = cols % 128 == 0
    last = (width, cols) if gather else (width, positions)
    slots = group if gather else 1
    dma = pltpu.SemaphoreType.DMA
    state = (heads, PACKED, E)
    vmem = pl.BlockSpec(memory_space=pltpu.VMEM)
    hbm = pl.BlockSpec(memory_space=pl.ANY)
    scratch = [
        pltpu.VMEM(tokens.shape, bf16),
        pltpu.VMEM((positions, wide), bf16),
        pltpu.VMEM(w_qk.shape, bf16),
        pltpu.VMEM(conv_qk.shape, f32),
        pltpu.VMEM(conv_v.shape, f32),
        pltpu.VMEM((positions, wide), bf16),
        pltpu.VMEM((positions, w_qk.shape[0]), bf16),
        pltpu.VMEM((n_fsdp, width, positions), f32),
        pltpu.VMEM((n_fsdp, width, positions), bf16),
        pltpu.VMEM((n_fsdp, width, positions), bf16),
        pltpu.VMEM((RIM, w_qk.shape[1]), f32),
        pltpu.VMEM((n_fsdp, RIM, w_qk.shape[1]), f32),
        pltpu.VMEM((w_qk.shape[1], positions), f32),
        pltpu.VMEM((RIM_V, wide), bf16),
        pltpu.VMEM((RIM_V + positions, wide), f32),
        pltpu.VMEM((positions, wide), bf16),
        pltpu.VMEM(state, bf16),
        pltpu.VMEM((n_ctx,) + state, bf16),
        pltpu.VMEM(state, f32),
        pltpu.VMEM(state, bf16),
        pltpu.VMEM((n_ctx,) + state, bf16),
        pltpu.VMEM(state, f32),
        pltpu.VMEM((positions, wide), bf16),
        pltpu.VMEM((positions + RIM, wide), f32),
        pltpu.VMEM((width, positions), f32),
        pltpu.VMEM((width, positions), f32),
        pltpu.VMEM((slots, positions, cols if gather else 128), bf16),
        pltpu.VMEM((slots, width, positions), bf16),
        dma((n_fsdp,)), dma((n_fsdp,)), dma((n_fsdp,)), dma((n_fsdp,)), dma, dma,
        dma((n_ctx, heads)), dma((n_ctx, heads)), dma((n_ctx, heads)), dma((n_ctx, heads)),
        dma, dma, dma, dma,
        dma((slots,)), dma((slots,)), dma((slots,)), dma((slots,)),
        dma((7,)), dma((n_ctx, heads)), dma((n_ctx, heads)),
    ]
    attended, grad_v, tail = pl.pallas_call(
        functools.partial(body, (n_ctx, n_fsdp, n_batch, gather)),
        out_shape=(
            jax.ShapeDtypeStruct((positions, wide), bf16),
            jax.ShapeDtypeStruct((positions, wide), bf16),
            jax.ShapeDtypeStruct(last, f32 if gather else bf16),
        ),
        in_specs=[hbm] * 6,
        out_specs=(vmem,) * 3,
        scratch_shapes=scratch,
        compiler_params=pltpu.CompilerParams(
            collective_id=0, has_side_effects=True, vmem_limit_bytes=56 * 2**20
        ),
    )(tokens, values[0], w_qk, conv_qk, conv_v, d_attn[0])
    if gather:
        grad_w = tail.T
    else:
        grad_w = lax.psum_scatter(
            dot(tail, tokens).T, ("ctx", "batch"), scatter_dimension=0, tiled=True
        ) * float(positions * group) ** (-0.5)
    return (attended[None], grad_v[None], grad_w)


def solution(mesh):
    in_specs = (
        P("batch", "ctx", None),
        P("batch", "ctx", "fsdp"),
        P("fsdp", None),
        P(None, "fsdp"),
        P(None, "fsdp"),
        P("batch", "ctx", "fsdp"),
    )
    out_specs = (P("batch", "ctx", "fsdp"), P("batch", "ctx", "fsdp"), P(("ctx", "batch"), "fsdp"))
    dims = (mesh.shape["ctx"], mesh.shape["fsdp"], mesh.shape["batch"])
    return jax.shard_map(
        functools.partial(shards, dims), mesh=mesh, in_specs=in_specs, out_specs=out_specs, check_vma=False
    )
```

```python
import functools

import jax
import jax.numpy as jnp
from jax import lax
from jax.experimental import pallas as pl
from jax.experimental.pallas import tpu as pltpu
from jax.sharding import PartitionSpec as P

F = 16
E = 256
CONV = 3
PACKED = 8 * F + F // 2 + 8 + F
RIM_V = 16
RIM = 8

eps_norm = 1e-05
MESH = pl.DeviceIdType.MESH
bf16, f32 = jnp.bfloat16, jnp.float32


def dot(a, b):
    return jnp.dot(a, b, preferred_element_type=f32)


def dot_nt(a, b):
    return lax.dot_general(a, b, (((1,), (1,)), ((), ())), preferred_element_type=f32)


def turned(rows, by):
    if by == 0:
        return rows
    return jnp.concatenate([rows[by:], rows[:by]], axis=0)


def features(vec):
    positions = vec.shape[1]
    rows = [vec * vec * (2.0 * F) ** (-0.5)]
    scaled = vec * F ** (-0.5)
    for by in range(1, F // 2):
        rows.append(scaled * turned(vec, by))
    rows.append(scaled[: F // 2] * vec[F // 2 :])
    first = lax.broadcasted_iota(jnp.int32, (8, positions), 0) == 0
    rows.append(jnp.where(first, 1.0, 0.0).astype(f32))
    rows.append(vec * F ** (-0.25))
    return jnp.concatenate(rows, axis=0)


def features_back(vec, up):
    half = F // 2
    total = vec * up[:F] * (2.0 * (2.0 * F) ** (-0.5))
    total = total + up[8 * F + half + 8 :] * F ** (-0.25)
    pairs = jnp.zeros_like(vec)
    for by in range(1, half):
        part = up[by * F : (by + 1) * F]
        pairs = pairs + turned(vec, by) * part + turned(vec * part, F - by)
    part = up[half * F : half * F + half]
    pairs = pairs + jnp.concatenate([vec[half:] * part, vec[:half] * part], axis=0)
    return total + pairs * F ** (-0.5)


def column_of(row):
    n = row.shape[1]
    same = lax.broadcasted_iota(jnp.int32, (n, n), 0) == lax.broadcasted_iota(jnp.int32, (n, n), 1)
    return jnp.sum(jnp.where(same, row, 0.0), axis=1, keepdims=True)


def body(
    dims, tokens_h, values_h, weights_h, conv_qk_h, conv_v_h, d_attn_h,
    attended, grad_v, grad_w,
    tokens, values, weights, conv_qk, conv_v, d_attn, own,
    part_f, part_t, part_in, rim_out, rim_in, rim_t, vrim_in, ext_v, conv_b,
    state_out, state_in, prior, grad_out, grad_in, later, mixed_b,
    dv_ext, dqk_out, dqk_in, x_in, dq_all,
    part_ss, part_rs, rim_ss, rim_rs, vrim_ss, vrim_rs, state_ss, state_rs,
    grad_ss, grad_rs, dv_ss, dv_rs, dqk_ss, dqk_rs, x_ss, x_rs, dq_ss, dq_rs,
    load_s, pass_s, back_s,
):
    n_ctx, n_fsdp, n_batch, gather = dims
    ctx, fsdp, batch = lax.axis_index("ctx"), lax.axis_index("fsdp"), lax.axis_index("batch")
    positions = tokens.shape[0]
    depth = weights.shape[0]
    width = conv_qk.shape[1]
    heads = width // (2 * F)
    wide = values.shape[1]
    group = n_ctx * n_batch
    me = ctx * n_batch + batch
    inner, outer = ctx > 0, ctx < n_ctx - 1

    def copy(src, dst, ss, rs, to):
        return pltpu.make_async_remote_copy(
            src_ref=src, dst_ref=dst, send_sem=ss, recv_sem=rs, device_id=to, device_id_type=MESH
        )

    bar = pltpu.get_barrier_semaphore()

    def greet(to):
        pl.semaphore_signal(bar, inc=1, device_id=to, device_id_type=MESH)

    for r in range(1, n_fsdp):
        greet((ctx, lax.rem(fsdp + r, n_fsdp), batch))
    if gather:
        for r in range(1, group):
            peer = lax.rem(me + r, group)
            greet((peer // n_batch, fsdp, lax.rem(peer, n_batch)))
        count = group - 1 + n_fsdp - 1
        same = range(1, n_fsdp)
    else:
        for r in range(1, n_ctx):
            greet((lax.rem(ctx + r, n_ctx), fsdp, batch))
        count = n_ctx - 1 + n_fsdp - 1
        same = range(1, n_fsdp)

    @pl.when(inner)
    def _():
        for r in same:
            greet((ctx - 1, lax.rem(fsdp + r, n_fsdp), batch))

    @pl.when(outer)
    def _():
        for r in same:
            greet((ctx + 1, lax.rem(fsdp + r, n_fsdp), batch))

    columns = pl.ds(pl.multiple_of(fsdp * depth, depth), depth)
    loads = [
        pltpu.make_async_copy(src, dst, load_s.at[i])
        for i, (src, dst) in enumerate(
            [
                (weights_h, weights), (tokens_h.at[:, columns], own), (values_h, values),
                (conv_v_h, conv_v), (conv_qk_h, conv_qk), (tokens_h, tokens), (d_attn_h, d_attn),
            ]
        )
    ]
    for load in loads:
        load.start()
    loads[0].wait()
    loads[1].wait()

    part = dot(own[...], weights[...])
    part_f[...] = part.T.reshape(part_f.shape)
    part_t[...] = part_f[...].astype(bf16)
    rim_out[...] = part[positions - RIM :]
    pl.semaphore_wait(
        bar, count + jnp.where(inner, n_fsdp - 1, 0) + jnp.where(outer, n_fsdp - 1, 0)
    )

    for load in loads[2:]:
        load.wait()

    def part_copy(r):
        peer = lax.rem(fsdp + r, n_fsdp)
        return copy(part_t.at[peer], part_in.at[fsdp], part_ss.at[r], part_rs.at[fsdp], (ctx, peer, batch))

    def rim_copy(r):
        peer = lax.rem(fsdp + r, n_fsdp)
        return copy(rim_out, rim_in.at[fsdp], rim_ss.at[r], rim_rs.at[fsdp], (ctx + 1, peer, batch))

    def vrim_copy():
        return copy(values.at[pl.ds(positions - RIM_V, RIM_V)], vrim_in, vrim_ss, vrim_rs, (ctx + 1, fsdp, batch))

    for r in range(1, n_fsdp):
        part_copy(r).start()

    @pl.when(outer)
    def _():
        for r in range(n_fsdp):
            rim_copy(r).start()
        vrim_copy().start()

    cols = tokens.shape[1] // group

    def x_copy(r):
        peer = lax.rem(me + r, group)
        return copy(
            tokens.at[:, pl.ds(pl.multiple_of(peer * cols, cols), cols)],
            x_in.at[me], x_ss.at[r], x_rs.at[me],
            (peer // n_batch, fsdp, lax.rem(peer, n_batch)),
        )

    pair = 2 if n_ctx % 2 == 0 else 1
    chip, core = ctx // pair, lax.rem(ctx, pair)
    mate = chip * pair + (pair - 1 - core)
    late = ctx < n_ctx // 2

    def x_start(first):
        for r in range(1, group):
            far = lax.rem(me + r, group) // (n_batch * pair) != chip
            held = jnp.logical_and(far, late)

            @pl.when(jnp.logical_not(held) if first else held)
            def _():
                x_copy(r).start()

    if gather:
        x_in[me] = tokens[:, pl.ds(pl.multiple_of(me * cols, cols), cols)]
        x_start(True)

    @pl.when(inner)
    def _():
        vrim_copy().wait_recv()
        ext_v[0:RIM_V] = vrim_in[...].astype(f32)

    @pl.when(jnp.logical_not(inner))
    def _():
        ext_v[0:RIM_V] = jnp.zeros((RIM_V, wide), f32)

    ext_v[RIM_V:] = values[...].astype(f32)
    running = conv_v[0:1] * ext_v[RIM_V:]
    for j in range(1, CONV):
        running = running + conv_v[j : j + 1] * ext_v[RIM_V - j : RIM_V - j + positions]
    conv_b[...] = running.astype(bf16)

    for r in range(1, n_fsdp):
        src = lax.rem(fsdp + r, n_fsdp)
        copy(part_in.at[src], part_in.at[src], part_ss.at[r], part_rs.at[src], (ctx, src, batch)).wait_recv()
    raw = part_f[fsdp]
    for r in range(1, n_fsdp):
        raw = raw + part_in[lax.rem(fsdp + r, n_fsdp)].astype(f32)
    raw = raw.astype(bf16).astype(f32)

    @pl.when(inner)
    def _():
        for s in range(n_fsdp):
            copy(rim_in.at[s], rim_in.at[s], rim_ss.at[s], rim_rs.at[s], (ctx - 1, s, batch)).wait_recv()
        rows = rim_in[0]
        for s in range(1, n_fsdp):
            rows = rows + rim_in[s]
        rows = rows.astype(bf16).astype(f32)
        block = jnp.concatenate([jnp.zeros((positions - RIM, rows.shape[1]), f32), rows], axis=0)
        rim_t[...] = block.T

    @pl.when(jnp.logical_not(inner))
    def _():
        rim_t[...] = jnp.zeros(rim_t.shape, f32)

    before = rim_t[pl.ds(pl.multiple_of(fsdp * width, width), width), :]
    lane = lax.broadcasted_iota(jnp.int32, (width, positions), 1)
    taps = [column_of(conv_qk[j : j + 1]) for j in range(CONV)]
    running = taps[0] * raw
    for j in range(1, CONV):
        moved = jnp.where(lane < j, pltpu.roll(before, j, 1), pltpu.roll(raw, j, 1))
        running = running + taps[j] * moved
    qk_t = running.astype(bf16).astype(f32)
    qk = qk_t.T.astype(bf16)

    q_t = [qk_t[h * 2 * F : h * 2 * F + F] for h in range(heads)]
    k_t = [qk_t[h * 2 * F + F : (h + 1) * 2 * F] for h in range(heads)]
    fk_t = [features(k) for k in k_t]

    def sent(out, into, ss, rs, h, to, i):
        return copy(out.at[h], into.at[ctx, h], ss.at[i, h], rs.at[ctx, h], (to, fsdp, batch))

    def send(out, into, ss, rs, h, sign, done):
        def act(c):
            c.wait_send() if done else c.start()

        if pair == 2:
            @pl.when(core == (0 if sign > 0 else 1))
            def _():
                act(sent(out, into, ss, rs, h, mate, 0))

        for i in range(1, n_ctx // pair):
            to = ctx + sign * pair * i

            @pl.when(jnp.logical_and(to >= 0, to < n_ctx))
            def _():
                act(sent(out, into, ss, rs, h, to, i))

    def passed(into, rs, ps, s, h):
        return copy(into.at[s, h], into.at[s, h], ps.at[s, h], rs.at[s, h], (mate, fsdp, batch))

    def relays(s, sign):
        if pair == 1:
            return s < 0
        there = s // pair < chip if sign > 0 else s // pair > chip
        return jnp.logical_and(there, core == s % pair)

    def receive(into, rs, ps, total, h, sign):
        for s in range(n_ctx):
            if pair == 2:
                @pl.when(relays(s, sign))
                def _():
                    passed(into, rs, ps, s, h).wait_recv()
                    passed(into, rs, ps, s, h).start()
        total[h] = jnp.zeros(total.shape[1:], f32)
        for s in range(n_ctx):
            wanted = s < ctx if sign > 0 else s > ctx
            plain = jnp.logical_and(wanted, jnp.logical_not(relays(s, sign))) if pair == 2 else wanted

            @pl.when(plain)
            def _():
                passed(into, rs, ps, s, h).wait_recv()

            @pl.when(wanted)
            def _():
                total[h] += into[s, h].astype(f32)

    def finish(out, into, ss, rs, ps, sign):
        for h in range(heads):
            send(out, into, ss, rs, h, sign, True)
            if pair == 2:
                for s in range(n_ctx):
                    @pl.when(relays(s, sign))
                    def _():
                        passed(into, rs, ps, s, h).wait_send()

    for h in range(heads):
        state_out[h] = dot(fk_t[h].astype(bf16), conv_b[:, h * E : (h + 1) * E]).astype(bf16)
        send(state_out, state_in, state_ss, state_rs, h, 1, False)
    fq_t = [features(q) for q in q_t]
    fq = [x.T.astype(bf16) for x in fq_t]
    fk = [x.T.astype(bf16) for x in fk_t]
    at_row = lax.broadcasted_iota(jnp.int32, (positions, positions), 0)
    at_col = lax.broadcasted_iota(jnp.int32, (positions, positions), 1)
    scores_t, kernels_t, local = [], [], []
    for h in range(heads):
        q, k = qk[:, h * 2 * F : h * 2 * F + F], qk[:, h * 2 * F + F : (h + 1) * 2 * F]
        score = dot(q, k_t[h].astype(bf16)) * F ** (-0.5)
        kernel = jnp.where(at_col <= at_row, 1.0 + score + 0.5 * score * score, 0.0).astype(bf16)
        local.append(dot(kernel, conv_b[:, h * E : (h + 1) * E]))
        score_t = dot(k, q_t[h].astype(bf16)) * F ** (-0.5)
        scores_t.append(score_t)
        kernels_t.append(
            jnp.where(at_row <= at_col, 1.0 + score_t + 0.5 * score_t * score_t, 0.0).astype(bf16)
        )

    if gather:
        x_start(False)

    prior_b = []
    for h in range(heads):
        lanes = slice(h * E, (h + 1) * E)
        receive(state_in, state_rs, pass_s, prior, h, 1)
        prior_b.append(prior[h].astype(bf16))
        mixed = local[h] + dot(fq[h], prior_b[h])
        inv = lax.rsqrt(jnp.mean(mixed * mixed, axis=-1, keepdims=True) + eps_norm)
        normed = mixed * inv
        attended[:, lanes] = normed.astype(bf16)
        g = d_attn[:, lanes].astype(f32)
        d_mixed = (inv * (g - normed * jnp.mean(g * normed, axis=-1, keepdims=True))).astype(bf16)
        mixed_b[:, lanes] = d_mixed
        grad_out[h] = dot(fq_t[h].astype(bf16), d_mixed).astype(bf16)
        send(grad_out, grad_in, grad_ss, grad_rs, h, -1, False)

    d_q, d_k, d_v = [], [], []
    for h in range(heads):
        lanes = slice(h * E, (h + 1) * E)
        d_mixed, value = mixed_b[:, lanes], conv_b[:, lanes]
        d_kernel_t = dot_nt(value, d_mixed)
        d_score_t = jnp.where(
            at_row <= at_col, d_kernel_t * (1.0 + scores_t[h]), 0.0
        ) * F ** (-0.5)
        d_score_t = d_score_t.astype(bf16)
        d_q.append(
            dot(k_t[h].astype(bf16), d_score_t) + features_back(q_t[h], dot_nt(prior_b[h], d_mixed))
        )
        d_k.append(dot_nt(q_t[h].astype(bf16), d_score_t))
        d_v.append(dot(kernels_t[h], d_mixed))

    rows, later_b = [], []
    for h in range(heads):
        receive(grad_in, grad_rs, back_s, later, h, -1)
        later_b.append(later[h].astype(bf16))
        back = features_back(k_t[h], dot_nt(later_b[h], conv_b[:, h * E : (h + 1) * E]))
        rows += [d_q[h], d_k[h] + back]
    d_qk_t = jnp.concatenate(rows, axis=0)

    def dq_copy(r):
        peer = lax.rem(me + r, group)
        return copy(
            dq_all.at[me], dq_all.at[me], dq_ss.at[r], dq_rs.at[me],
            (peer // n_batch, fsdp, lax.rem(peer, n_batch)),
        )

    def dqk_copy():
        return copy(dqk_out, dqk_in, dqk_ss, dqk_rs, (ctx - 1, fsdp, batch))

    if gather:
        dq_all[me] = d_qk_t.astype(bf16)
        for r in range(1, group):
            dq_copy(r).start()
    else:
        dqk_out[...] = d_qk_t

        @pl.when(inner)
        def _():
            dqk_copy().start()

    def dv_copy():
        return copy(
            dv_ext.at[pl.ds(0, RIM)], dv_ext.at[pl.ds(positions, RIM)], dv_ss, dv_rs, (ctx - 1, fsdp, batch)
        )

    for h in range(heads):
        dv_ext[0:positions, h * E : (h + 1) * E] = d_v[h] + dot(fk[h], later_b[h])

    @pl.when(inner)
    def _():
        dv_copy().start()

    def convolve_back(here, after):
        running = taps[0] * here
        for j in range(1, CONV):
            moved = pltpu.roll(here, positions - j, 1)
            rim = 0.0 if after is None else pltpu.roll(after, positions - j, 1)
            running = running + taps[j] * jnp.where(lane >= positions - j, rim, moved)
        return running.astype(bf16)

    if not gather:
        @pl.when(outer)
        def _():
            dqk_copy().wait_recv()

        @pl.when(jnp.logical_not(outer))
        def _():
            dqk_in[...] = jnp.zeros(dqk_in.shape, f32)

        grad_w[...] = convolve_back(d_qk_t, dqk_in[...])

    @pl.when(outer)
    def _():
        dv_copy().wait_recv()

    @pl.when(jnp.logical_not(outer))
    def _():
        dv_ext[positions:] = jnp.zeros((RIM, wide), f32)

    running = conv_v[0:1] * dv_ext[0:positions]
    for j in range(1, CONV):
        running = running + conv_v[j : j + 1] * dv_ext[j : j + positions]
    grad_v[...] = running.astype(bf16)

    if gather:
        for r in range(1, group):
            src = lax.rem(me + r, group)
            to = (src // n_batch, fsdp, lax.rem(src, n_batch))
            copy(x_in.at[src], x_in.at[src], x_ss.at[r], x_rs.at[src], to).wait_recv()
            copy(dq_all.at[src], dq_all.at[src], dq_ss.at[r], dq_rs.at[src], to).wait_recv()
        blocks = [dq_all[s].astype(f32) for s in range(group)]
        d_pre = [
            convolve_back(blocks[s], blocks[s + n_batch] if s + n_batch < group else None)
            for s in range(group)
        ]
        total = dot(jnp.concatenate(d_pre, axis=1), x_in[...].reshape(group * positions, cols))
        grad_w[...] = total * float(positions * group) ** (-0.5)
        for r in range(1, group):
            x_copy(r).wait_send()
            dq_copy(r).wait_send()

    for r in range(1, n_fsdp):
        part_copy(r).wait_send()

    @pl.when(outer)
    def _():
        for r in range(n_fsdp):
            rim_copy(r).wait_send()
        vrim_copy().wait_send()

    @pl.when(inner)
    def _():
        if not gather:
            dqk_copy().wait_send()
        dv_copy().wait_send()

    finish(state_out, state_in, state_ss, state_rs, pass_s, 1)
    finish(grad_out, grad_in, grad_ss, grad_rs, back_s, -1)


def write(*refs):
    *blocks, sems = refs
    n = len(blocks) // 2
    copies = [pltpu.make_async_copy(blocks[i], blocks[n + i], sems.at[i]) for i in range(n)]
    for c in copies:
        c.start()
    for c in copies:
        c.wait()


def shards(dims, inputs, values, w_qk, conv_qk, conv_v, d_attn):
    n_ctx, n_fsdp, n_batch = dims
    tokens = inputs[0]
    positions, model = tokens.shape
    wide = values.shape[2]
    width = conv_qk.shape[1]
    heads = width // (2 * F)
    group = n_ctx * n_batch
    cols = model // group
    gather = cols % 128 == 0
    last = (width, cols) if gather else (width, positions)
    slots = group if gather else 1
    dma = pltpu.SemaphoreType.DMA
    state = (heads, PACKED, E)
    vmem = pl.BlockSpec(memory_space=pltpu.VMEM)
    hbm = pl.BlockSpec(memory_space=pl.ANY)
    scratch = [
        pltpu.VMEM(tokens.shape, bf16),
        pltpu.VMEM((positions, wide), bf16),
        pltpu.VMEM(w_qk.shape, bf16),
        pltpu.VMEM(conv_qk.shape, f32),
        pltpu.VMEM(conv_v.shape, f32),
        pltpu.VMEM((positions, wide), bf16),
        pltpu.VMEM((positions, w_qk.shape[0]), bf16),
        pltpu.VMEM((n_fsdp, width, positions), f32),
        pltpu.VMEM((n_fsdp, width, positions), bf16),
        pltpu.VMEM((n_fsdp, width, positions), bf16),
        pltpu.VMEM((RIM, w_qk.shape[1]), f32),
        pltpu.VMEM((n_fsdp, RIM, w_qk.shape[1]), f32),
        pltpu.VMEM((w_qk.shape[1], positions), f32),
        pltpu.VMEM((RIM_V, wide), bf16),
        pltpu.VMEM((RIM_V + positions, wide), f32),
        pltpu.VMEM((positions, wide), bf16),
        pltpu.VMEM(state, bf16),
        pltpu.VMEM((n_ctx,) + state, bf16),
        pltpu.VMEM(state, f32),
        pltpu.VMEM(state, bf16),
        pltpu.VMEM((n_ctx,) + state, bf16),
        pltpu.VMEM(state, f32),
        pltpu.VMEM((positions, wide), bf16),
        pltpu.VMEM((positions + RIM, wide), f32),
        pltpu.VMEM((width, positions), f32),
        pltpu.VMEM((width, positions), f32),
        pltpu.VMEM((slots, positions, cols if gather else 128), bf16),
        pltpu.VMEM((slots, width, positions), bf16),
        dma((n_fsdp,)), dma((n_fsdp,)), dma((n_fsdp,)), dma((n_fsdp,)), dma, dma,
        dma((n_ctx, heads)), dma((n_ctx, heads)), dma((n_ctx, heads)), dma((n_ctx, heads)),
        dma, dma, dma, dma,
        dma((slots,)), dma((slots,)), dma((slots,)), dma((slots,)),
        dma((7,)), dma((n_ctx, heads)), dma((n_ctx, heads)),
    ]
    place = pltpu.VMEM if gather else jax.ShapeDtypeStruct
    attended, grad_v, tail = pl.pallas_call(
        functools.partial(body, (n_ctx, n_fsdp, n_batch, gather)),
        out_shape=(
            place((positions, wide), bf16),
            place((positions, wide), bf16),
            place(last, f32 if gather else bf16),
        ),
        in_specs=[hbm] * 6,
        out_specs=(vmem,) * 3,
        scratch_shapes=scratch,
        compiler_params=pltpu.CompilerParams(
            collective_id=0, has_side_effects=True, vmem_limit_bytes=56 * 2**20
        ),
    )(tokens, values[0], w_qk, conv_qk, conv_v, d_attn[0])
    if gather:
        blocks = (attended, grad_v, tail)
        attended, grad_v, tail = pl.pallas_call(
            write,
            out_shape=tuple(jax.ShapeDtypeStruct(x.shape, x.dtype) for x in blocks),
            in_specs=[vmem] * 3,
            out_specs=(hbm,) * 3,
            scratch_shapes=[dma((3,))],
        )(*blocks)
        grad_w = tail.T
    else:
        grad_w = lax.psum_scatter(
            dot(tail, tokens).T, ("ctx", "batch"), scatter_dimension=0, tiled=True
        ) * float(positions * group) ** (-0.5)
    return (attended[None], grad_v[None], grad_w)


def solution(mesh):
    in_specs = (
        P("batch", "ctx", None),
        P("batch", "ctx", "fsdp"),
        P("fsdp", None),
        P(None, "fsdp"),
        P(None, "fsdp"),
        P("batch", "ctx", "fsdp"),
    )
    out_specs = (P("batch", "ctx", "fsdp"), P("batch", "ctx", "fsdp"), P(("ctx", "batch"), "fsdp"))
    dims = (mesh.shape["ctx"], mesh.shape["fsdp"], mesh.shape["batch"])
    return jax.shard_map(
        functools.partial(shards, dims), mesh=mesh, in_specs=in_specs, out_specs=out_specs, check_vma=False
    )
```

```python
import functools

import jax
import jax.numpy as jnp
from jax import lax
from jax.experimental import pallas as pl
from jax.experimental.pallas import tpu as pltpu
from jax.sharding import PartitionSpec as P

F = 16
E = 256
CONV = 3
PACKED = 8 * F + F // 2 + 8 + F
RIM_V = 16
RIM = 8

eps_norm = 1e-05
MESH = pl.DeviceIdType.MESH
bf16, f32 = jnp.bfloat16, jnp.float32


def dot(a, b):
    return jnp.dot(a, b, preferred_element_type=f32)


def dot_nt(a, b):
    return lax.dot_general(a, b, (((1,), (1,)), ((), ())), preferred_element_type=f32)


def turned(rows, by):
    if by == 0:
        return rows
    return jnp.concatenate([rows[by:], rows[:by]], axis=0)


def features(vec):
    positions = vec.shape[1]
    rows = [vec * vec * (2.0 * F) ** (-0.5)]
    scaled = vec * F ** (-0.5)
    for by in range(1, F // 2):
        rows.append(scaled * turned(vec, by))
    rows.append(scaled[: F // 2] * vec[F // 2 :])
    first = lax.broadcasted_iota(jnp.int32, (8, positions), 0) == 0
    rows.append(jnp.where(first, 1.0, 0.0).astype(f32))
    rows.append(vec * F ** (-0.25))
    return jnp.concatenate(rows, axis=0)


def features_back(vec, up):
    half = F // 2
    total = vec * up[:F] * (2.0 * (2.0 * F) ** (-0.5))
    total = total + up[8 * F + half + 8 :] * F ** (-0.25)
    pairs = jnp.zeros_like(vec)
    for by in range(1, half):
        part = up[by * F : (by + 1) * F]
        pairs = pairs + turned(vec, by) * part + turned(vec * part, F - by)
    part = up[half * F : half * F + half]
    pairs = pairs + jnp.concatenate([vec[half:] * part, vec[:half] * part], axis=0)
    return total + pairs * F ** (-0.5)


def column_of(row):
    n = row.shape[1]
    same = lax.broadcasted_iota(jnp.int32, (n, n), 0) == lax.broadcasted_iota(jnp.int32, (n, n), 1)
    return jnp.sum(jnp.where(same, row, 0.0), axis=1, keepdims=True)


def body(
    dims, tokens_h, values_h, weights_h, conv_qk_h, conv_v_h, d_attn_h,
    attended, grad_v, grad_w,
    tokens, values, weights, conv_qk, conv_v, d_attn, own,
    part_f, part_t, part_in, rim_out, rim_in, rim_t, vrim_in, ext_v, conv_b,
    state_out, state_in, prior, grad_out, grad_in, later, mixed_b,
    dv_ext, dqk_out, dqk_in, x_in, dq_all, v_in, k_out, k_in, mixed_f, pulled,
    part_ss, part_rs, rim_ss, rim_rs, vrim_ss, vrim_rs, state_ss, state_rs,
    grad_ss, grad_rs, dv_ss, dv_rs, dqk_ss, dqk_rs, x_ss, x_rs, dq_ss, dq_rs,
    load_s, pass_s, back_s, v_ss, v_rs, v_ps, k_ss, k_rs,
):
    n_ctx, n_fsdp, n_batch, gather = dims
    ctx, fsdp, batch = lax.axis_index("ctx"), lax.axis_index("fsdp"), lax.axis_index("batch")
    positions = tokens.shape[0]
    depth = weights.shape[0]
    width = conv_qk.shape[1]
    heads = width // (2 * F)
    wide = values.shape[1]
    group = n_ctx * n_batch
    me = ctx * n_batch + batch
    inner, outer = ctx > 0, ctx < n_ctx - 1

    def copy(src, dst, ss, rs, to):
        return pltpu.make_async_remote_copy(
            src_ref=src, dst_ref=dst, send_sem=ss, recv_sem=rs, device_id=to, device_id_type=MESH
        )

    bar = pltpu.get_barrier_semaphore()

    def greet(to):
        pl.semaphore_signal(bar, inc=1, device_id=to, device_id_type=MESH)

    for r in range(1, n_fsdp):
        greet((ctx, lax.rem(fsdp + r, n_fsdp), batch))
    if gather:
        for r in range(1, group):
            peer = lax.rem(me + r, group)
            greet((peer // n_batch, fsdp, lax.rem(peer, n_batch)))
        count = group - 1 + n_fsdp - 1
        same = range(1, n_fsdp)
    else:
        for r in range(1, n_ctx):
            greet((lax.rem(ctx + r, n_ctx), fsdp, batch))
        count = n_ctx - 1 + n_fsdp - 1
        same = range(1, n_fsdp)

    @pl.when(inner)
    def _():
        for r in same:
            greet((ctx - 1, lax.rem(fsdp + r, n_fsdp), batch))

    @pl.when(outer)
    def _():
        for r in same:
            greet((ctx + 1, lax.rem(fsdp + r, n_fsdp), batch))

    columns = pl.ds(pl.multiple_of(fsdp * depth, depth), depth)
    loads = [
        pltpu.make_async_copy(src, dst, load_s.at[i])
        for i, (src, dst) in enumerate(
            [
                (weights_h, weights), (tokens_h.at[:, columns], own), (values_h, values),
                (conv_v_h, conv_v), (conv_qk_h, conv_qk), (tokens_h, tokens), (d_attn_h, d_attn),
            ]
        )
    ]
    for load in loads:
        load.start()
    loads[0].wait()
    loads[1].wait()

    part = dot(own[...], weights[...])
    part_f[...] = part.T.reshape(part_f.shape)
    part_t[...] = part_f[...].astype(bf16)
    rim_out[...] = part[positions - RIM :]
    pl.semaphore_wait(
        bar, count + jnp.where(inner, n_fsdp - 1, 0) + jnp.where(outer, n_fsdp - 1, 0)
    )

    for load in loads[2:]:
        load.wait()

    def part_copy(r):
        peer = lax.rem(fsdp + r, n_fsdp)
        return copy(part_t.at[peer], part_in.at[fsdp], part_ss.at[r], part_rs.at[fsdp], (ctx, peer, batch))

    def rim_copy(r):
        peer = lax.rem(fsdp + r, n_fsdp)
        return copy(rim_out, rim_in.at[fsdp], rim_ss.at[r], rim_rs.at[fsdp], (ctx + 1, peer, batch))

    def vrim_copy():
        return copy(values.at[pl.ds(positions - RIM_V, RIM_V)], vrim_in, vrim_ss, vrim_rs, (ctx + 1, fsdp, batch))

    for r in range(1, n_fsdp):
        part_copy(r).start()

    @pl.when(outer)
    def _():
        for r in range(n_fsdp):
            rim_copy(r).start()
        vrim_copy().start()

    cols = tokens.shape[1] // group

    def x_copy(r):
        peer = lax.rem(me + r, group)
        return copy(
            tokens.at[:, pl.ds(pl.multiple_of(peer * cols, cols), cols)],
            x_in.at[me], x_ss.at[r], x_rs.at[me],
            (peer // n_batch, fsdp, lax.rem(peer, n_batch)),
        )

    pair = 2 if n_ctx % 2 == 0 else 1
    chip, core = ctx // pair, lax.rem(ctx, pair)
    mate = chip * pair + (pair - 1 - core)
    late = ctx < n_ctx // 2

    def x_start(first):
        for r in range(1, group):
            far = lax.rem(me + r, group) // (n_batch * pair) != chip
            held = jnp.logical_and(far, late)

            @pl.when(jnp.logical_not(held) if first else held)
            def _():
                x_copy(r).start()

    if gather:
        x_in[me] = tokens[:, pl.ds(pl.multiple_of(me * cols, cols), cols)]
        x_start(True)

    def sent(out, into, ss, rs, h, to, i):
        return copy(out if out is conv_b else out.at[h], into.at[ctx, h], ss.at[i, h], rs.at[ctx, h], (to, fsdp, batch))

    def send(out, into, ss, rs, h, sign, done):
        def act(c):
            c.wait_send() if done else c.start()

        if pair == 2:
            @pl.when(core == (0 if sign > 0 else 1))
            def _():
                act(sent(out, into, ss, rs, h, mate, 0))

        for i in range(1, n_ctx // pair):
            to = ctx + sign * pair * i

            @pl.when(jnp.logical_and(to >= 0, to < n_ctx))
            def _():
                act(sent(out, into, ss, rs, h, to, i))

    def passed(into, rs, ps, s, h):
        return copy(into.at[s, h], into.at[s, h], ps.at[s, h], rs.at[s, h], (mate, fsdp, batch))

    def relays(s, sign):
        if pair == 1:
            return s < 0
        there = s // pair < chip if sign > 0 else s // pair > chip
        return jnp.logical_and(there, core == s % pair)

    def receive(into, rs, ps, total, h, sign):
        for s in range(n_ctx):
            if pair == 2:
                @pl.when(relays(s, sign))
                def _():
                    passed(into, rs, ps, s, h).wait_recv()
                    passed(into, rs, ps, s, h).start()
        total[h] = jnp.zeros(total.shape[1:], f32)
        for s in range(n_ctx):
            wanted = s < ctx if sign > 0 else s > ctx
            plain = jnp.logical_and(wanted, jnp.logical_not(relays(s, sign))) if pair == 2 else wanted

            @pl.when(plain)
            def _():
                passed(into, rs, ps, s, h).wait_recv()

            @pl.when(wanted)
            def _():
                total[h] += into[s, h].astype(f32)

    def finish(out, into, ss, rs, ps, sign):
        for h in range(into.shape[1]):
            send(out, into, ss, rs, h, sign, True)
            if pair == 2:
                for s in range(n_ctx):
                    @pl.when(relays(s, sign))
                    def _():
                        passed(into, rs, ps, s, h).wait_send()

    @pl.when(inner)
    def _():
        vrim_copy().wait_recv()
        ext_v[0:RIM_V] = vrim_in[...].astype(f32)

    @pl.when(jnp.logical_not(inner))
    def _():
        ext_v[0:RIM_V] = jnp.zeros((RIM_V, wide), f32)

    ext_v[RIM_V:] = values[...].astype(f32)
    running = conv_v[0:1] * ext_v[RIM_V:]
    for j in range(1, CONV):
        running = running + conv_v[j : j + 1] * ext_v[RIM_V - j : RIM_V - j + positions]
    conv_b[...] = running.astype(bf16)
    if gather:
        send(conv_b, v_in, v_ss, v_rs, 0, 1, False)

    for r in range(1, n_fsdp):
        src = lax.rem(fsdp + r, n_fsdp)
        copy(part_in.at[src], part_in.at[src], part_ss.at[r], part_rs.at[src], (ctx, src, batch)).wait_recv()
    raw = part_f[fsdp]
    for r in range(1, n_fsdp):
        raw = raw + part_in[lax.rem(fsdp + r, n_fsdp)].astype(f32)
    raw = raw.astype(bf16).astype(f32)

    @pl.when(inner)
    def _():
        for s in range(n_fsdp):
            copy(rim_in.at[s], rim_in.at[s], rim_ss.at[s], rim_rs.at[s], (ctx - 1, s, batch)).wait_recv()
        rows = rim_in[0]
        for s in range(1, n_fsdp):
            rows = rows + rim_in[s]
        rows = rows.astype(bf16).astype(f32)
        block = jnp.concatenate([jnp.zeros((positions - RIM, rows.shape[1]), f32), rows], axis=0)
        rim_t[...] = block.T

    @pl.when(jnp.logical_not(inner))
    def _():
        rim_t[...] = jnp.zeros(rim_t.shape, f32)

    before = rim_t[pl.ds(pl.multiple_of(fsdp * width, width), width), :]
    lane = lax.broadcasted_iota(jnp.int32, (width, positions), 1)
    taps = [column_of(conv_qk[j : j + 1]) for j in range(CONV)]
    running = taps[0] * raw
    for j in range(1, CONV):
        moved = jnp.where(lane < j, pltpu.roll(before, j, 1), pltpu.roll(raw, j, 1))
        running = running + taps[j] * moved
    qk_t = running.astype(bf16).astype(f32)
    qk = qk_t.T.astype(bf16)

    q_t = [qk_t[h * 2 * F : h * 2 * F + F] for h in range(heads)]
    k_t = [qk_t[h * 2 * F + F : (h + 1) * 2 * F] for h in range(heads)]
    fk_t = [features(k) for k in k_t]

    def k_copy(r):
        return copy(k_out, k_in.at[ctx], k_ss.at[r], k_rs.at[ctx], (ctx + r, fsdp, batch))

    if gather:
        k_out[...] = qk_t.astype(bf16)
        for r in range(1, n_ctx):
            @pl.when(ctx + r < n_ctx)
            def _():
                k_copy(r).start()
        x_start(False)
        for i in range(n_ctx):
            if pair == 2:
                @pl.when(relays(i, 1))
                def _():
                    passed(v_in, v_rs, v_ps, i, 0).wait_recv()
                    passed(v_in, v_rs, v_ps, i, 0).start()
    for h in range(0 if gather else heads):
        state_out[h] = dot(fk_t[h].astype(bf16), conv_b[:, h * E : (h + 1) * E]).astype(bf16)
        send(state_out, state_in, state_ss, state_rs, h, 1, False)
    fq_t = [features(q) for q in q_t]
    fk = [x.T.astype(bf16) for x in fk_t]
    at_row = lax.broadcasted_iota(jnp.int32, (positions, positions), 0)
    at_col = lax.broadcasted_iota(jnp.int32, (positions, positions), 1)
    scores_t, kernels_t, local = [], [], []
    for h in range(heads):
        q, k = qk[:, h * 2 * F : h * 2 * F + F], qk[:, h * 2 * F + F : (h + 1) * 2 * F]
        score = dot(q, k_t[h].astype(bf16)) * F ** (-0.5)
        kernel = jnp.where(at_col <= at_row, 1.0 + score + 0.5 * score * score, 0.0).astype(bf16)
        local.append(dot(kernel, conv_b[:, h * E : (h + 1) * E]))
        score_t = dot(k, q_t[h].astype(bf16)) * F ** (-0.5)
        scores_t.append(score_t)
        kernels_t.append(
            jnp.where(at_row <= at_col, 1.0 + score_t + 0.5 * score_t * score_t, 0.0).astype(bf16)
        )

    def earlier(act):
        for i in range(n_ctx - 1):
            @pl.when(i < ctx)
            def _():
                for h in range(heads):
                    q = qk[:, h * 2 * F : h * 2 * F + F]
                    k = k_in[i, h * 2 * F + F : (h + 1) * 2 * F]
                    act(i, h, k, dot(q, k) * F ** (-0.5), v_in[i, 0, :, h * E : (h + 1) * E])

    def mix(i, h, k, score, value):
        kernel = (1.0 + score + 0.5 * score * score).astype(bf16)
        mixed_f[:, h * E : (h + 1) * E] += dot(kernel, value)

    def pull(i, h, k, score, value):
        d_kernel = dot_nt(mixed_b[:, h * E : (h + 1) * E], value)
        d_score = (d_kernel * (1.0 + score) * F ** (-0.5)).astype(bf16)
        pulled[h] += dot_nt(k, d_score)

    if gather:
        for h in range(heads):
            mixed_f[:, h * E : (h + 1) * E] = local[h]
        for i in range(n_ctx - 1):
            @pl.when(i < ctx)
            def _():
                copy(k_in.at[i], k_in.at[i], k_ss.at[i], k_rs.at[i], (i, fsdp, batch)).wait_recv()

            @pl.when(jnp.logical_and(i < ctx, jnp.logical_not(relays(i, 1))) if pair == 2 else i < ctx)
            def _():
                passed(v_in, v_rs, v_ps, i, 0).wait_recv()
        earlier(mix)

    prior_b = []
    for h in range(heads):
        lanes = slice(h * E, (h + 1) * E)
        if gather:
            mixed = mixed_f[:, lanes]
        else:
            receive(state_in, state_rs, pass_s, prior, h, 1)
            prior_b.append(prior[h].astype(bf16))
            mixed = local[h] + dot(fq_t[h].T.astype(bf16), prior_b[h])
        inv = lax.rsqrt(jnp.mean(mixed * mixed, axis=-1, keepdims=True) + eps_norm)
        normed = mixed * inv
        attended[:, lanes] = normed.astype(bf16)
        g = d_attn[:, lanes].astype(f32)
        d_mixed = (inv * (g - normed * jnp.mean(g * normed, axis=-1, keepdims=True))).astype(bf16)
        mixed_b[:, lanes] = d_mixed
        grad_out[h] = dot(fq_t[h].astype(bf16), d_mixed).astype(bf16)
        send(grad_out, grad_in, grad_ss, grad_rs, h, -1, False)

    d_q, d_k, d_v = [], [], []
    if gather:
        pulled[...] = jnp.zeros(pulled.shape, f32)
        earlier(pull)
    for h in range(heads):
        lanes = slice(h * E, (h + 1) * E)
        d_mixed, value = mixed_b[:, lanes], conv_b[:, lanes]
        d_kernel_t = dot_nt(value, d_mixed)
        d_score_t = jnp.where(
            at_row <= at_col, d_kernel_t * (1.0 + scores_t[h]), 0.0
        ) * F ** (-0.5)
        d_score_t = d_score_t.astype(bf16)
        d_q.append(
            dot(k_t[h].astype(bf16), d_score_t)
            + (pulled[h] if gather else features_back(q_t[h], dot_nt(prior_b[h], d_mixed)))
        )
        d_k.append(dot_nt(q_t[h].astype(bf16), d_score_t))
        d_v.append(dot(kernels_t[h], d_mixed))

    rows, later_b = [], []
    for h in range(heads):
        receive(grad_in, grad_rs, back_s, later, h, -1)
        later_b.append(later[h].astype(bf16))
        back = features_back(k_t[h], dot_nt(later_b[h], conv_b[:, h * E : (h + 1) * E]))
        rows += [d_q[h], d_k[h] + back]
    d_qk_t = jnp.concatenate(rows, axis=0)

    def dq_copy(r):
        peer = lax.rem(me + r, group)
        return copy(
            dq_all.at[me], dq_all.at[me], dq_ss.at[r], dq_rs.at[me],
            (peer // n_batch, fsdp, lax.rem(peer, n_batch)),
        )

    def dqk_copy():
        return copy(dqk_out, dqk_in, dqk_ss, dqk_rs, (ctx - 1, fsdp, batch))

    if gather:
        dq_all[me] = d_qk_t.astype(bf16)
        for r in range(1, group):
            dq_copy(r).start()
    else:
        dqk_out[...] = d_qk_t

        @pl.when(inner)
        def _():
            dqk_copy().start()

    def dv_copy():
        return copy(
            dv_ext.at[pl.ds(0, RIM)], dv_ext.at[pl.ds(positions, RIM)], dv_ss, dv_rs, (ctx - 1, fsdp, batch)
        )

    for h in range(heads):
        dv_ext[0:positions, h * E : (h + 1) * E] = d_v[h] + dot(fk[h], later_b[h])

    @pl.when(inner)
    def _():
        dv_copy().start()

    def convolve_back(here, after):
        running = taps[0] * here
        for j in range(1, CONV):
            moved = pltpu.roll(here, positions - j, 1)
            rim = 0.0 if after is None else pltpu.roll(after, positions - j, 1)
            running = running + taps[j] * jnp.where(lane >= positions - j, rim, moved)
        return running.astype(bf16)

    if not gather:
        @pl.when(outer)
        def _():
            dqk_copy().wait_recv()

        @pl.when(jnp.logical_not(outer))
        def _():
            dqk_in[...] = jnp.zeros(dqk_in.shape, f32)

        grad_w[...] = convolve_back(d_qk_t, dqk_in[...])

    @pl.when(outer)
    def _():
        dv_copy().wait_recv()

    @pl.when(jnp.logical_not(outer))
    def _():
        dv_ext[positions:] = jnp.zeros((RIM, wide), f32)

    running = conv_v[0:1] * dv_ext[0:positions]
    for j in range(1, CONV):
        running = running + conv_v[j : j + 1] * dv_ext[j : j + positions]
    grad_v[...] = running.astype(bf16)

    if gather:
        for r in range(1, group):
            src = lax.rem(me + r, group)
            to = (src // n_batch, fsdp, lax.rem(src, n_batch))
            copy(x_in.at[src], x_in.at[src], x_ss.at[r], x_rs.at[src], to).wait_recv()
            copy(dq_all.at[src], dq_all.at[src], dq_ss.at[r], dq_rs.at[src], to).wait_recv()
        blocks = [dq_all[s].astype(f32) for s in range(group)]
        d_pre = [
            convolve_back(blocks[s], blocks[s + n_batch] if s + n_batch < group else None)
            for s in range(group)
        ]
        total = dot(jnp.concatenate(d_pre, axis=1), x_in[...].reshape(group * positions, cols))
        grad_w[...] = total * float(positions * group) ** (-0.5)
        for r in range(1, group):
            x_copy(r).wait_send()
            dq_copy(r).wait_send()

    for r in range(1, n_fsdp):
        part_copy(r).wait_send()

    @pl.when(outer)
    def _():
        for r in range(n_fsdp):
            rim_copy(r).wait_send()
        vrim_copy().wait_send()

    @pl.when(inner)
    def _():
        if not gather:
            dqk_copy().wait_send()
        dv_copy().wait_send()

    if gather:
        finish(conv_b, v_in, v_ss, v_rs, v_ps, 1)
        for r in range(1, n_ctx):
            @pl.when(ctx + r < n_ctx)
            def _():
                k_copy(r).wait_send()
    else:
        finish(state_out, state_in, state_ss, state_rs, pass_s, 1)
    finish(grad_out, grad_in, grad_ss, grad_rs, back_s, -1)


def shards(dims, inputs, values, w_qk, conv_qk, conv_v, d_attn):
    n_ctx, n_fsdp, n_batch = dims
    tokens = inputs[0]
    positions, model = tokens.shape
    wide = values.shape[2]
    width = conv_qk.shape[1]
    heads = width // (2 * F)
    group = n_ctx * n_batch
    cols = model // group
    gather = cols % 128 == 0
    last = (width, cols) if gather else (width, positions)
    slots = group if gather else 1
    dma = pltpu.SemaphoreType.DMA
    state = (heads, PACKED, E)
    vmem = pl.BlockSpec(memory_space=pltpu.VMEM)
    hbm = pl.BlockSpec(memory_space=pl.ANY)
    scratch = [
        pltpu.VMEM(tokens.shape, bf16),
        pltpu.VMEM((positions, wide), bf16),
        pltpu.VMEM(w_qk.shape, bf16),
        pltpu.VMEM(conv_qk.shape, f32),
        pltpu.VMEM(conv_v.shape, f32),
        pltpu.VMEM((positions, wide), bf16),
        pltpu.VMEM((positions, w_qk.shape[0]), bf16),
        pltpu.VMEM((n_fsdp, width, positions), f32),
        pltpu.VMEM((n_fsdp, width, positions), bf16),
        pltpu.VMEM((n_fsdp, width, positions), bf16),
        pltpu.VMEM((RIM, w_qk.shape[1]), f32),
        pltpu.VMEM((n_fsdp, RIM, w_qk.shape[1]), f32),
        pltpu.VMEM((w_qk.shape[1], positions), f32),
        pltpu.VMEM((RIM_V, wide), bf16),
        pltpu.VMEM((RIM_V + positions, wide), f32),
        pltpu.VMEM((positions, wide), bf16),
        pltpu.VMEM(state, bf16),
        pltpu.VMEM((n_ctx,) + state, bf16),
        pltpu.VMEM(state, f32),
        pltpu.VMEM(state, bf16),
        pltpu.VMEM((n_ctx,) + state, bf16),
        pltpu.VMEM(state, f32),
        pltpu.VMEM((positions, wide), bf16),
        pltpu.VMEM((positions + RIM, wide), f32),
        pltpu.VMEM((width, positions), f32),
        pltpu.VMEM((width, positions), f32),
        pltpu.VMEM((slots, positions, cols if gather else 128), bf16),
        pltpu.VMEM((slots, width, positions), bf16),
        pltpu.VMEM((n_ctx, 1, positions, wide), bf16),
        pltpu.VMEM((width, positions), bf16),
        pltpu.VMEM((n_ctx, width, positions), bf16),
        pltpu.VMEM((positions, wide), f32),
        pltpu.VMEM((heads, F, positions), f32),
        dma((n_fsdp,)), dma((n_fsdp,)), dma((n_fsdp,)), dma((n_fsdp,)), dma, dma,
        dma((n_ctx, heads)), dma((n_ctx, heads)), dma((n_ctx, heads)), dma((n_ctx, heads)),
        dma, dma, dma, dma,
        dma((slots,)), dma((slots,)), dma((slots,)), dma((slots,)),
        dma((7,)), dma((n_ctx, heads)), dma((n_ctx, heads)),
        dma((n_ctx, 1)), dma((n_ctx, 1)), dma((n_ctx, 1)), dma((n_ctx,)), dma((n_ctx,)),
    ]
    place = pltpu.VMEM if gather else jax.ShapeDtypeStruct
    attended, grad_v, tail = pl.pallas_call(
        functools.partial(body, (n_ctx, n_fsdp, n_batch, gather)),
        out_shape=(
            place((positions, wide), bf16),
            place((positions, wide), bf16),
            place(last, f32 if gather else bf16),
        ),
        in_specs=[hbm] * 6,
        out_specs=(vmem,) * 3,
        scratch_shapes=scratch,
        compiler_params=pltpu.CompilerParams(
            collective_id=0, has_side_effects=True, vmem_limit_bytes=56 * 2**20
        ),
    )(tokens, values[0], w_qk, conv_qk, conv_v, d_attn[0])
    if gather:
        grad_w = tail.T
    else:
        grad_w = lax.psum_scatter(
            dot(tail, tokens).T, ("ctx", "batch"), scatter_dimension=0, tiled=True
        ) * float(positions * group) ** (-0.5)
    return (attended[None], grad_v[None], grad_w)


def solution(mesh):
    in_specs = (
        P("batch", "ctx", None),
        P("batch", "ctx", "fsdp"),
        P("fsdp", None),
        P(None, "fsdp"),
        P(None, "fsdp"),
        P("batch", "ctx", "fsdp"),
    )
    out_specs = (P("batch", "ctx", "fsdp"), P("batch", "ctx", "fsdp"), P(("ctx", "batch"), "fsdp"))
    dims = (mesh.shape["ctx"], mesh.shape["fsdp"], mesh.shape["batch"])
    return jax.shard_map(
        functools.partial(shards, dims), mesh=mesh, in_specs=in_specs, out_specs=out_specs, check_vma=False
    )
```

```python
import functools

import jax
import jax.numpy as jnp
from jax import lax
from jax.experimental import pallas as pl
from jax.experimental.pallas import tpu as pltpu
from jax.sharding import PartitionSpec as P

F = 16
E = 256
CONV = 3
PACKED = 8 * F + F // 2 + 8 + F
RIM_V = 16
RIM = 8

eps_norm = 1e-05
MESH = pl.DeviceIdType.MESH
bf16, f32 = jnp.bfloat16, jnp.float32


def dot(a, b):
    return jnp.dot(a, b, preferred_element_type=f32)


def dot_nt(a, b):
    return lax.dot_general(a, b, (((1,), (1,)), ((), ())), preferred_element_type=f32)


def turned(rows, by):
    if by == 0:
        return rows
    return jnp.concatenate([rows[by:], rows[:by]], axis=0)


def features(vec):
    positions = vec.shape[1]
    rows = [vec * vec * (2.0 * F) ** (-0.5)]
    scaled = vec * F ** (-0.5)
    for by in range(1, F // 2):
        rows.append(scaled * turned(vec, by))
    rows.append(scaled[: F // 2] * vec[F // 2 :])
    first = lax.broadcasted_iota(jnp.int32, (8, positions), 0) == 0
    rows.append(jnp.where(first, 1.0, 0.0).astype(f32))
    rows.append(vec * F ** (-0.25))
    return jnp.concatenate(rows, axis=0)


def features_back(vec, up):
    half = F // 2
    total = vec * up[:F] * (2.0 * (2.0 * F) ** (-0.5))
    total = total + up[8 * F + half + 8 :] * F ** (-0.25)
    pairs = jnp.zeros_like(vec)
    for by in range(1, half):
        part = up[by * F : (by + 1) * F]
        pairs = pairs + turned(vec, by) * part + turned(vec * part, F - by)
    part = up[half * F : half * F + half]
    pairs = pairs + jnp.concatenate([vec[half:] * part, vec[:half] * part], axis=0)
    return total + pairs * F ** (-0.5)


def column_of(row):
    n = row.shape[1]
    same = lax.broadcasted_iota(jnp.int32, (n, n), 0) == lax.broadcasted_iota(jnp.int32, (n, n), 1)
    return jnp.sum(jnp.where(same, row, 0.0), axis=1, keepdims=True)


def body(
    dims, tokens_h, values_h, weights_h, conv_qk_h, conv_v_h, d_attn_h,
    attended, grad_v, grad_w,
    tokens, values, weights, conv_qk, conv_v, d_attn, own,
    part_f, part_t, part_in, rim_out, rim_in, rim_t, vrim_in, ext_v, conv_b,
    state_out, state_in, prior, grad_out, grad_in, later, mixed_b,
    dv_ext, dqk_out, dqk_in, x_in, dq_all, v_in, k_out, k_in, mixed_f, pulled,
    part_ss, part_rs, rim_ss, rim_rs, vrim_ss, vrim_rs, state_ss, state_rs,
    grad_ss, grad_rs, dv_ss, dv_rs, dqk_ss, dqk_rs, x_ss, x_rs, dq_ss, dq_rs,
    load_s, pass_s, back_s, v_ss, v_rs, v_ps, k_ss, k_rs,
):
    n_ctx, n_fsdp, n_batch, gather = dims
    ctx, fsdp, batch = lax.axis_index("ctx"), lax.axis_index("fsdp"), lax.axis_index("batch")
    positions = tokens.shape[0]
    depth = weights.shape[0]
    width = conv_qk.shape[1]
    heads = width // (2 * F)
    wide = values.shape[1]
    group = n_ctx * n_batch
    me = ctx * n_batch + batch
    inner, outer = ctx > 0, ctx < n_ctx - 1

    def copy(src, dst, ss, rs, to):
        return pltpu.make_async_remote_copy(
            src_ref=src, dst_ref=dst, send_sem=ss, recv_sem=rs, device_id=to, device_id_type=MESH
        )

    bar = pltpu.get_barrier_semaphore()

    def greet(to):
        pl.semaphore_signal(bar, inc=1, device_id=to, device_id_type=MESH)

    for r in range(1, n_fsdp):
        greet((ctx, lax.rem(fsdp + r, n_fsdp), batch))
    if gather:
        for r in range(1, group):
            peer = lax.rem(me + r, group)
            greet((peer // n_batch, fsdp, lax.rem(peer, n_batch)))
        count = group - 1 + n_fsdp - 1
        same = range(1, n_fsdp)
    else:
        for r in range(1, n_ctx):
            greet((lax.rem(ctx + r, n_ctx), fsdp, batch))
        count = n_ctx - 1 + n_fsdp - 1
        same = range(1, n_fsdp)

    @pl.when(inner)
    def _():
        for r in same:
            greet((ctx - 1, lax.rem(fsdp + r, n_fsdp), batch))

    @pl.when(outer)
    def _():
        for r in same:
            greet((ctx + 1, lax.rem(fsdp + r, n_fsdp), batch))

    columns = pl.ds(pl.multiple_of(fsdp * depth, depth), depth)
    loads = [
        pltpu.make_async_copy(src, dst, load_s.at[i])
        for i, (src, dst) in enumerate(
            [
                (weights_h, weights), (tokens_h.at[:, columns], own), (values_h, values),
                (conv_v_h, conv_v), (conv_qk_h, conv_qk), (tokens_h, tokens), (d_attn_h, d_attn),
            ]
        )
    ]
    for load in loads:
        load.start()
    loads[0].wait()
    loads[1].wait()

    part = dot(own[...], weights[...])
    part_f[...] = part.T.reshape(part_f.shape)
    part_t[...] = part_f[...].astype(bf16)
    rim_out[...] = part[positions - RIM :]
    pl.semaphore_wait(
        bar, count + jnp.where(inner, n_fsdp - 1, 0) + jnp.where(outer, n_fsdp - 1, 0)
    )

    for load in loads[2:]:
        load.wait()

    def part_copy(r):
        peer = lax.rem(fsdp + r, n_fsdp)
        return copy(part_t.at[peer], part_in.at[fsdp], part_ss.at[r], part_rs.at[fsdp], (ctx, peer, batch))

    def rim_copy(r):
        peer = lax.rem(fsdp + r, n_fsdp)
        return copy(rim_out, rim_in.at[fsdp], rim_ss.at[r], rim_rs.at[fsdp], (ctx + 1, peer, batch))

    def vrim_copy():
        return copy(values.at[pl.ds(positions - RIM_V, RIM_V)], vrim_in, vrim_ss, vrim_rs, (ctx + 1, fsdp, batch))

    for r in range(1, n_fsdp):
        part_copy(r).start()

    @pl.when(outer)
    def _():
        for r in range(n_fsdp):
            rim_copy(r).start()
        vrim_copy().start()

    cols = tokens.shape[1] // group

    def x_copy(r):
        peer = lax.rem(me + r, group)
        return copy(
            tokens.at[:, pl.ds(pl.multiple_of(peer * cols, cols), cols)],
            x_in.at[me], x_ss.at[r], x_rs.at[me],
            (peer // n_batch, fsdp, lax.rem(peer, n_batch)),
        )

    pair = 2 if n_ctx % 2 == 0 else 1
    chip, core = ctx // pair, lax.rem(ctx, pair)
    mate = chip * pair + (pair - 1 - core)
    late = ctx < n_ctx // 2

    def x_start(stage):
        for r in range(1, group):
            peer = lax.rem(me + r, group)
            far = peer // (n_batch * pair) != chip
            aside = jnp.logical_and(far, lax.rem(peer, n_batch) != batch)
            turn = jnp.where(late, jnp.where(far, 1, 0), jnp.where(aside, 2, 0))

            @pl.when(turn == stage)
            def _():
                x_copy(r).start()

    if gather:
        x_in[me] = tokens[:, pl.ds(pl.multiple_of(me * cols, cols), cols)]
        x_start(0)

    def sent(out, into, ss, rs, h, to, i):
        return copy(out if out is conv_b else out.at[h], into.at[ctx, h], ss.at[i, h], rs.at[ctx, h], (to, fsdp, batch))

    def send(out, into, ss, rs, h, sign, done):
        def act(c):
            c.wait_send() if done else c.start()

        if pair == 2:
            @pl.when(core == (0 if sign > 0 else 1))
            def _():
                act(sent(out, into, ss, rs, h, mate, 0))

        for i in range(1, n_ctx // pair):
            to = ctx + sign * pair * i

            @pl.when(jnp.logical_and(to >= 0, to < n_ctx))
            def _():
                act(sent(out, into, ss, rs, h, to, i))

    def passed(into, rs, ps, s, h):
        return copy(into.at[s, h], into.at[s, h], ps.at[s, h], rs.at[s, h], (mate, fsdp, batch))

    def relays(s, sign):
        if pair == 1:
            return s < 0
        there = s // pair < chip if sign > 0 else s // pair > chip
        return jnp.logical_and(there, core == s % pair)

    def receive(into, rs, ps, total, h, sign):
        for s in range(n_ctx):
            if pair == 2:
                @pl.when(relays(s, sign))
                def _():
                    passed(into, rs, ps, s, h).wait_recv()
                    passed(into, rs, ps, s, h).start()
        total[h] = jnp.zeros(total.shape[1:], f32)
        for s in range(n_ctx):
            wanted = s < ctx if sign > 0 else s > ctx
            plain = jnp.logical_and(wanted, jnp.logical_not(relays(s, sign))) if pair == 2 else wanted

            @pl.when(plain)
            def _():
                passed(into, rs, ps, s, h).wait_recv()

            @pl.when(wanted)
            def _():
                total[h] += into[s, h].astype(f32)

    def finish(out, into, ss, rs, ps, sign):
        for h in range(into.shape[1]):
            send(out, into, ss, rs, h, sign, True)
            if pair == 2:
                for s in range(n_ctx):
                    @pl.when(relays(s, sign))
                    def _():
                        passed(into, rs, ps, s, h).wait_send()

    @pl.when(inner)
    def _():
        vrim_copy().wait_recv()
        ext_v[0:RIM_V] = vrim_in[...].astype(f32)

    @pl.when(jnp.logical_not(inner))
    def _():
        ext_v[0:RIM_V] = jnp.zeros((RIM_V, wide), f32)

    ext_v[RIM_V:] = values[...].astype(f32)
    running = conv_v[0:1] * ext_v[RIM_V:]
    for j in range(1, CONV):
        running = running + conv_v[j : j + 1] * ext_v[RIM_V - j : RIM_V - j + positions]
    conv_b[...] = running.astype(bf16)
    if gather:
        send(conv_b, v_in, v_ss, v_rs, 0, 1, False)

    for r in range(1, n_fsdp):
        src = lax.rem(fsdp + r, n_fsdp)
        copy(part_in.at[src], part_in.at[src], part_ss.at[r], part_rs.at[src], (ctx, src, batch)).wait_recv()
    raw = part_f[fsdp]
    for r in range(1, n_fsdp):
        raw = raw + part_in[lax.rem(fsdp + r, n_fsdp)].astype(f32)
    raw = raw.astype(bf16).astype(f32)

    @pl.when(inner)
    def _():
        for s in range(n_fsdp):
            copy(rim_in.at[s], rim_in.at[s], rim_ss.at[s], rim_rs.at[s], (ctx - 1, s, batch)).wait_recv()
        rows = rim_in[0]
        for s in range(1, n_fsdp):
            rows = rows + rim_in[s]
        rows = rows.astype(bf16).astype(f32)
        block = jnp.concatenate([jnp.zeros((positions - RIM, rows.shape[1]), f32), rows], axis=0)
        rim_t[...] = block.T

    @pl.when(jnp.logical_not(inner))
    def _():
        rim_t[...] = jnp.zeros(rim_t.shape, f32)

    before = rim_t[pl.ds(pl.multiple_of(fsdp * width, width), width), :]
    lane = lax.broadcasted_iota(jnp.int32, (width, positions), 1)
    taps = [column_of(conv_qk[j : j + 1]) for j in range(CONV)]
    running = taps[0] * raw
    for j in range(1, CONV):
        moved = jnp.where(lane < j, pltpu.roll(before, j, 1), pltpu.roll(raw, j, 1))
        running = running + taps[j] * moved
    qk_t = running.astype(bf16).astype(f32)
    qk = qk_t.T.astype(bf16)

    q_t = [qk_t[h * 2 * F : h * 2 * F + F] for h in range(heads)]
    k_t = [qk_t[h * 2 * F + F : (h + 1) * 2 * F] for h in range(heads)]
    fk_t = [features(k) for k in k_t]

    def k_copy(r):
        return copy(k_out, k_in.at[ctx], k_ss.at[r], k_rs.at[ctx], (ctx + r, fsdp, batch))

    if gather:
        k_out[...] = qk_t.astype(bf16)
        for r in range(1, n_ctx):
            @pl.when(ctx + r < n_ctx)
            def _():
                k_copy(r).start()
        x_start(1)
        for i in range(n_ctx):
            if pair == 2:
                @pl.when(relays(i, 1))
                def _():
                    passed(v_in, v_rs, v_ps, i, 0).wait_recv()
                    passed(v_in, v_rs, v_ps, i, 0).start()
    for h in range(0 if gather else heads):
        state_out[h] = dot(fk_t[h].astype(bf16), conv_b[:, h * E : (h + 1) * E]).astype(bf16)
        send(state_out, state_in, state_ss, state_rs, h, 1, False)
    fq_t = [features(q) for q in q_t]
    fk = [x.T.astype(bf16) for x in fk_t]
    at_row = lax.broadcasted_iota(jnp.int32, (positions, positions), 0)
    at_col = lax.broadcasted_iota(jnp.int32, (positions, positions), 1)
    scores_t, kernels_t, local = [], [], []
    for h in range(heads):
        q, k = qk[:, h * 2 * F : h * 2 * F + F], qk[:, h * 2 * F + F : (h + 1) * 2 * F]
        score = dot(q, k_t[h].astype(bf16)) * F ** (-0.5)
        kernel = jnp.where(at_col <= at_row, 1.0 + score + 0.5 * score * score, 0.0).astype(bf16)
        local.append(dot(kernel, conv_b[:, h * E : (h + 1) * E]))
        score_t = dot(k, q_t[h].astype(bf16)) * F ** (-0.5)
        scores_t.append(score_t)
        kernels_t.append(
            jnp.where(at_row <= at_col, 1.0 + score_t + 0.5 * score_t * score_t, 0.0).astype(bf16)
        )

    def earlier(act):
        for i in range(n_ctx - 1):
            @pl.when(i < ctx)
            def _():
                for h in range(heads):
                    q = qk[:, h * 2 * F : h * 2 * F + F]
                    k = k_in[i, h * 2 * F + F : (h + 1) * 2 * F]
                    act(i, h, k, dot(q, k) * F ** (-0.5), v_in[i, 0, :, h * E : (h + 1) * E])

    def mix(i, h, k, score, value):
        kernel = (1.0 + score + 0.5 * score * score).astype(bf16)
        mixed_f[:, h * E : (h + 1) * E] += dot(kernel, value)

    def pull(i, h, k, score, value):
        d_kernel = dot_nt(mixed_b[:, h * E : (h + 1) * E], value)
        d_score = (d_kernel * (1.0 + score) * F ** (-0.5)).astype(bf16)
        pulled[h] += dot_nt(k, d_score)

    if gather:
        for h in range(heads):
            mixed_f[:, h * E : (h + 1) * E] = local[h]
        for i in range(n_ctx - 1):
            @pl.when(i < ctx)
            def _():
                copy(k_in.at[i], k_in.at[i], k_ss.at[i], k_rs.at[i], (i, fsdp, batch)).wait_recv()

            @pl.when(jnp.logical_and(i < ctx, jnp.logical_not(relays(i, 1))) if pair == 2 else i < ctx)
            def _():
                passed(v_in, v_rs, v_ps, i, 0).wait_recv()
        earlier(mix)

    prior_b = []
    for h in range(heads):
        lanes = slice(h * E, (h + 1) * E)
        if gather:
            mixed = mixed_f[:, lanes]
        else:
            receive(state_in, state_rs, pass_s, prior, h, 1)
            prior_b.append(prior[h].astype(bf16))
            mixed = local[h] + dot(fq_t[h].T.astype(bf16), prior_b[h])
        inv = lax.rsqrt(jnp.mean(mixed * mixed, axis=-1, keepdims=True) + eps_norm)
        normed = mixed * inv
        attended[:, lanes] = normed.astype(bf16)
        g = d_attn[:, lanes].astype(f32)
        d_mixed = (inv * (g - normed * jnp.mean(g * normed, axis=-1, keepdims=True))).astype(bf16)
        mixed_b[:, lanes] = d_mixed
        grad_out[h] = dot(fq_t[h].astype(bf16), d_mixed).astype(bf16)
        send(grad_out, grad_in, grad_ss, grad_rs, h, -1, False)

    d_q, d_k, d_v = [], [], []
    if gather:
        x_start(2)
        pulled[...] = jnp.zeros(pulled.shape, f32)
        earlier(pull)
    for h in range(heads):
        lanes = slice(h * E, (h + 1) * E)
        d_mixed, value = mixed_b[:, lanes], conv_b[:, lanes]
        d_kernel_t = dot_nt(value, d_mixed)
        d_score_t = jnp.where(
            at_row <= at_col, d_kernel_t * (1.0 + scores_t[h]), 0.0
        ) * F ** (-0.5)
        d_score_t = d_score_t.astype(bf16)
        d_q.append(
            dot(k_t[h].astype(bf16), d_score_t)
            + (pulled[h] if gather else features_back(q_t[h], dot_nt(prior_b[h], d_mixed)))
        )
        d_k.append(dot_nt(q_t[h].astype(bf16), d_score_t))
        d_v.append(dot(kernels_t[h], d_mixed))

    rows, later_b = [], []
    for h in range(heads):
        receive(grad_in, grad_rs, back_s, later, h, -1)
        later_b.append(later[h].astype(bf16))
        back = features_back(k_t[h], dot_nt(later_b[h], conv_b[:, h * E : (h + 1) * E]))
        rows += [d_q[h], d_k[h] + back]
    d_qk_t = jnp.concatenate(rows, axis=0)

    def dq_copy(r):
        peer = lax.rem(me + r, group)
        return copy(
            dq_all.at[me], dq_all.at[me], dq_ss.at[r], dq_rs.at[me],
            (peer // n_batch, fsdp, lax.rem(peer, n_batch)),
        )

    def dqk_copy():
        return copy(dqk_out, dqk_in, dqk_ss, dqk_rs, (ctx - 1, fsdp, batch))

    if gather:
        dq_all[me] = d_qk_t.astype(bf16)
        for r in range(1, group):
            dq_copy(r).start()
    else:
        dqk_out[...] = d_qk_t

        @pl.when(inner)
        def _():
            dqk_copy().start()

    def dv_copy():
        return copy(
            dv_ext.at[pl.ds(0, RIM)], dv_ext.at[pl.ds(positions, RIM)], dv_ss, dv_rs, (ctx - 1, fsdp, batch)
        )

    for h in range(heads):
        dv_ext[0:positions, h * E : (h + 1) * E] = d_v[h] + dot(fk[h], later_b[h])

    @pl.when(inner)
    def _():
        dv_copy().start()

    def convolve_back(here, after):
        running = taps[0] * here
        for j in range(1, CONV):
            moved = pltpu.roll(here, positions - j, 1)
            rim = 0.0 if after is None else pltpu.roll(after, positions - j, 1)
            running = running + taps[j] * jnp.where(lane >= positions - j, rim, moved)
        return running.astype(bf16)

    if not gather:
        @pl.when(outer)
        def _():
            dqk_copy().wait_recv()

        @pl.when(jnp.logical_not(outer))
        def _():
            dqk_in[...] = jnp.zeros(dqk_in.shape, f32)

        grad_w[...] = convolve_back(d_qk_t, dqk_in[...])

    @pl.when(outer)
    def _():
        dv_copy().wait_recv()

    @pl.when(jnp.logical_not(outer))
    def _():
        dv_ext[positions:] = jnp.zeros((RIM, wide), f32)

    running = conv_v[0:1] * dv_ext[0:positions]
    for j in range(1, CONV):
        running = running + conv_v[j : j + 1] * dv_ext[j : j + positions]
    grad_v[...] = running.astype(bf16)

    if gather:
        for r in range(1, group):
            src = lax.rem(me + r, group)
            to = (src // n_batch, fsdp, lax.rem(src, n_batch))
            copy(x_in.at[src], x_in.at[src], x_ss.at[r], x_rs.at[src], to).wait_recv()
            copy(dq_all.at[src], dq_all.at[src], dq_ss.at[r], dq_rs.at[src], to).wait_recv()
        blocks = [dq_all[s].astype(f32) for s in range(group)]
        d_pre = [
            convolve_back(blocks[s], blocks[s + n_batch] if s + n_batch < group else None)
            for s in range(group)
        ]
        total = dot(jnp.concatenate(d_pre, axis=1), x_in[...].reshape(group * positions, cols))
        grad_w[...] = total * float(positions * group) ** (-0.5)
        for r in range(1, group):
            x_copy(r).wait_send()
            dq_copy(r).wait_send()

    for r in range(1, n_fsdp):
        part_copy(r).wait_send()

    @pl.when(outer)
    def _():
        for r in range(n_fsdp):
            rim_copy(r).wait_send()
        vrim_copy().wait_send()

    @pl.when(inner)
    def _():
        if not gather:
            dqk_copy().wait_send()
        dv_copy().wait_send()

    if gather:
        finish(conv_b, v_in, v_ss, v_rs, v_ps, 1)
        for r in range(1, n_ctx):
            @pl.when(ctx + r < n_ctx)
            def _():
                k_copy(r).wait_send()
    else:
        finish(state_out, state_in, state_ss, state_rs, pass_s, 1)
    finish(grad_out, grad_in, grad_ss, grad_rs, back_s, -1)


def shards(dims, inputs, values, w_qk, conv_qk, conv_v, d_attn):
    n_ctx, n_fsdp, n_batch = dims
    tokens = inputs[0]
    positions, model = tokens.shape
    wide = values.shape[2]
    width = conv_qk.shape[1]
    heads = width // (2 * F)
    group = n_ctx * n_batch
    cols = model // group
    gather = cols % 128 == 0
    last = (width, cols) if gather else (width, positions)
    slots = group if gather else 1
    dma = pltpu.SemaphoreType.DMA
    state = (heads, PACKED, E)
    vmem = pl.BlockSpec(memory_space=pltpu.VMEM)
    hbm = pl.BlockSpec(memory_space=pl.ANY)
    scratch = [
        pltpu.VMEM(tokens.shape, bf16),
        pltpu.VMEM((positions, wide), bf16),
        pltpu.VMEM(w_qk.shape, bf16),
        pltpu.VMEM(conv_qk.shape, f32),
        pltpu.VMEM(conv_v.shape, f32),
        pltpu.VMEM((positions, wide), bf16),
        pltpu.VMEM((positions, w_qk.shape[0]), bf16),
        pltpu.VMEM((n_fsdp, width, positions), f32),
        pltpu.VMEM((n_fsdp, width, positions), bf16),
        pltpu.VMEM((n_fsdp, width, positions), bf16),
        pltpu.VMEM((RIM, w_qk.shape[1]), f32),
        pltpu.VMEM((n_fsdp, RIM, w_qk.shape[1]), f32),
        pltpu.VMEM((w_qk.shape[1], positions), f32),
        pltpu.VMEM((RIM_V, wide), bf16),
        pltpu.VMEM((RIM_V + positions, wide), f32),
        pltpu.VMEM((positions, wide), bf16),
        pltpu.VMEM(state, bf16),
        pltpu.VMEM((n_ctx,) + state, bf16),
        pltpu.VMEM(state, f32),
        pltpu.VMEM(state, bf16),
        pltpu.VMEM((n_ctx,) + state, bf16),
        pltpu.VMEM(state, f32),
        pltpu.VMEM((positions, wide), bf16),
        pltpu.VMEM((positions + RIM, wide), f32),
        pltpu.VMEM((width, positions), f32),
        pltpu.VMEM((width, positions), f32),
        pltpu.VMEM((slots, positions, cols if gather else 128), bf16),
        pltpu.VMEM((slots, width, positions), bf16),
        pltpu.VMEM((n_ctx, 1, positions, wide), bf16),
        pltpu.VMEM((width, positions), bf16),
        pltpu.VMEM((n_ctx, width, positions), bf16),
        pltpu.VMEM((positions, wide), f32),
        pltpu.VMEM((heads, F, positions), f32),
        dma((n_fsdp,)), dma((n_fsdp,)), dma((n_fsdp,)), dma((n_fsdp,)), dma, dma,
        dma((n_ctx, heads)), dma((n_ctx, heads)), dma((n_ctx, heads)), dma((n_ctx, heads)),
        dma, dma, dma, dma,
        dma((slots,)), dma((slots,)), dma((slots,)), dma((slots,)),
        dma((7,)), dma((n_ctx, heads)), dma((n_ctx, heads)),
        dma((n_ctx, 1)), dma((n_ctx, 1)), dma((n_ctx, 1)), dma((n_ctx,)), dma((n_ctx,)),
    ]
    place = pltpu.VMEM if gather else jax.ShapeDtypeStruct
    attended, grad_v, tail = pl.pallas_call(
        functools.partial(body, (n_ctx, n_fsdp, n_batch, gather)),
        out_shape=(
            place((positions, wide), bf16),
            place((positions, wide), bf16),
            place(last, f32 if gather else bf16),
        ),
        in_specs=[hbm] * 6,
        out_specs=(vmem,) * 3,
        scratch_shapes=scratch,
        compiler_params=pltpu.CompilerParams(
            collective_id=0, has_side_effects=True, vmem_limit_bytes=56 * 2**20
        ),
    )(tokens, values[0], w_qk, conv_qk, conv_v, d_attn[0])
    if gather:
        grad_w = tail.T
    else:
        grad_w = lax.psum_scatter(
            dot(tail, tokens).T, ("ctx", "batch"), scatter_dimension=0, tiled=True
        ) * float(positions * group) ** (-0.5)
    return (attended[None], grad_v[None], grad_w)


def solution(mesh):
    in_specs = (
        P("batch", "ctx", None),
        P("batch", "ctx", "fsdp"),
        P("fsdp", None),
        P(None, "fsdp"),
        P(None, "fsdp"),
        P("batch", "ctx", "fsdp"),
    )
    out_specs = (P("batch", "ctx", "fsdp"), P("batch", "ctx", "fsdp"), P(("ctx", "batch"), "fsdp"))
    dims = (mesh.shape["ctx"], mesh.shape["fsdp"], mesh.shape["batch"])
    return jax.shard_map(
        functools.partial(shards, dims), mesh=mesh, in_specs=in_specs, out_specs=out_specs, check_vma=False
    )
```

```python
import functools

import jax
import jax.numpy as jnp
from jax import lax
from jax.experimental import pallas as pl
from jax.experimental.pallas import tpu as pltpu
from jax.sharding import PartitionSpec as P

F = 16
E = 256
CONV = 3
PACKED = 8 * F + F // 2 + 8 + F
RIM_V = 16
RIM = 8

eps_norm = 1e-05
MESH = pl.DeviceIdType.MESH
bf16, f32 = jnp.bfloat16, jnp.float32


def dot(a, b):
    return jnp.dot(a, b, preferred_element_type=f32)


def dot_nt(a, b):
    return lax.dot_general(a, b, (((1,), (1,)), ((), ())), preferred_element_type=f32)


def turned(rows, by):
    if by == 0:
        return rows
    return jnp.concatenate([rows[by:], rows[:by]], axis=0)


def features(vec):
    positions = vec.shape[1]
    rows = [vec * vec * (2.0 * F) ** (-0.5)]
    scaled = vec * F ** (-0.5)
    for by in range(1, F // 2):
        rows.append(scaled * turned(vec, by))
    rows.append(scaled[: F // 2] * vec[F // 2 :])
    first = lax.broadcasted_iota(jnp.int32, (8, positions), 0) == 0
    rows.append(jnp.where(first, 1.0, 0.0).astype(f32))
    rows.append(vec * F ** (-0.25))
    return jnp.concatenate(rows, axis=0)


def features_back(vec, up):
    half = F // 2
    total = vec * up[:F] * (2.0 * (2.0 * F) ** (-0.5))
    total = total + up[8 * F + half + 8 :] * F ** (-0.25)
    pairs = jnp.zeros_like(vec)
    for by in range(1, half):
        part = up[by * F : (by + 1) * F]
        pairs = pairs + turned(vec, by) * part + turned(vec * part, F - by)
    part = up[half * F : half * F + half]
    pairs = pairs + jnp.concatenate([vec[half:] * part, vec[:half] * part], axis=0)
    return total + pairs * F ** (-0.5)


def column_of(row):
    n = row.shape[1]
    same = lax.broadcasted_iota(jnp.int32, (n, n), 0) == lax.broadcasted_iota(jnp.int32, (n, n), 1)
    return jnp.sum(jnp.where(same, row, 0.0), axis=1, keepdims=True)


def body(
    dims, tokens_h, values_h, weights_h, conv_qk_h, conv_v_h, d_attn_h,
    attended, grad_v, grad_w,
    tokens, values, weights, conv_qk, conv_v, d_attn, own,
    part_f, part_t, part_in, rim_out, rim_in, rim_t, vrim_in, ext_v, conv_b,
    state_out, state_in, prior, grad_out, grad_in, later, mixed_b,
    dv_ext, dqk_out, dqk_in, x_in, dq_all, v_in, k_out, k_in, mixed_f, pulled,
    part_ss, part_rs, rim_ss, rim_rs, vrim_ss, vrim_rs, state_ss, state_rs,
    grad_ss, grad_rs, dv_ss, dv_rs, dqk_ss, dqk_rs, x_ss, x_rs, dq_ss, dq_rs,
    load_s, pass_s, back_s, v_ss, v_rs, v_ps, k_ss, k_rs,
):
    n_ctx, n_fsdp, n_batch, gather = dims
    ctx, fsdp, batch = lax.axis_index("ctx"), lax.axis_index("fsdp"), lax.axis_index("batch")
    positions = tokens.shape[0]
    depth = weights.shape[0]
    width = conv_qk.shape[1]
    heads = width // (2 * F)
    wide = values.shape[1]
    group = n_ctx * n_batch
    me = ctx * n_batch + batch
    inner, outer = ctx > 0, ctx < n_ctx - 1

    def copy(src, dst, ss, rs, to):
        return pltpu.make_async_remote_copy(
            src_ref=src, dst_ref=dst, send_sem=ss, recv_sem=rs, device_id=to, device_id_type=MESH
        )

    bar = pltpu.get_barrier_semaphore()

    def greet(to):
        pl.semaphore_signal(bar, inc=1, device_id=to, device_id_type=MESH)

    for r in range(1, n_fsdp):
        greet((ctx, lax.rem(fsdp + r, n_fsdp), batch))
    if gather:
        for r in range(1, group):
            peer = lax.rem(me + r, group)
            greet((peer // n_batch, fsdp, lax.rem(peer, n_batch)))
        count = group - 1 + n_fsdp - 1
        same = range(1, n_fsdp)
    else:
        for r in range(1, n_ctx):
            greet((lax.rem(ctx + r, n_ctx), fsdp, batch))
        count = n_ctx - 1 + n_fsdp - 1
        same = range(1, n_fsdp)

    @pl.when(inner)
    def _():
        for r in same:
            greet((ctx - 1, lax.rem(fsdp + r, n_fsdp), batch))

    @pl.when(outer)
    def _():
        for r in same:
            greet((ctx + 1, lax.rem(fsdp + r, n_fsdp), batch))

    columns = pl.ds(pl.multiple_of(fsdp * depth, depth), depth)
    loads = [
        pltpu.make_async_copy(src, dst, load_s.at[i])
        for i, (src, dst) in enumerate(
            [
                (weights_h, weights), (tokens_h.at[:, columns], own), (values_h, values),
                (conv_v_h, conv_v), (conv_qk_h, conv_qk), (tokens_h, tokens), (d_attn_h, d_attn),
            ]
        )
    ]
    for load in loads:
        load.start()
    loads[0].wait()
    loads[1].wait()

    part = dot(own[...], weights[...])
    part_f[...] = part.T.reshape(part_f.shape)
    part_t[...] = part_f[...].astype(bf16)
    rim_out[...] = part[positions - RIM :]
    pl.semaphore_wait(
        bar, count + jnp.where(inner, n_fsdp - 1, 0) + jnp.where(outer, n_fsdp - 1, 0)
    )

    for load in loads[2:]:
        load.wait()

    def part_copy(r):
        peer = lax.rem(fsdp + r, n_fsdp)
        return copy(part_t.at[peer], part_in.at[fsdp], part_ss.at[r], part_rs.at[fsdp], (ctx, peer, batch))

    def rim_copy(r):
        peer = lax.rem(fsdp + r, n_fsdp)
        return copy(rim_out, rim_in.at[fsdp], rim_ss.at[r], rim_rs.at[fsdp], (ctx + 1, peer, batch))

    def vrim_copy():
        return copy(values.at[pl.ds(positions - RIM_V, RIM_V)], vrim_in, vrim_ss, vrim_rs, (ctx + 1, fsdp, batch))

    for r in range(1, n_fsdp):
        part_copy(r).start()

    @pl.when(outer)
    def _():
        for r in range(n_fsdp):
            rim_copy(r).start()
        vrim_copy().start()

    cols = tokens.shape[1] // group

    def x_copy(r):
        peer = lax.rem(me + r, group)
        return copy(
            tokens.at[:, pl.ds(pl.multiple_of(peer * cols, cols), cols)],
            x_in.at[me], x_ss.at[r], x_rs.at[me],
            (peer // n_batch, fsdp, lax.rem(peer, n_batch)),
        )

    pair = 2 if n_ctx % 2 == 0 else 1
    chip, core = ctx // pair, lax.rem(ctx, pair)
    mate = chip * pair + (pair - 1 - core)
    late = ctx < n_ctx // 2

    def x_start(stage):
        for r in range(1, group):
            peer = lax.rem(me + r, group)
            far = peer // (n_batch * pair) != chip
            aside = jnp.logical_and(far, lax.rem(peer, n_batch) != batch)
            turn = jnp.where(late, jnp.where(far, 1, 0), jnp.where(aside, 2, jnp.where(far, 1, 0)))

            @pl.when(turn == stage)
            def _():
                x_copy(r).start()

    if gather:
        x_in[me] = tokens[:, pl.ds(pl.multiple_of(me * cols, cols), cols)]
        x_start(0)

    def sent(out, into, ss, rs, h, to, i):
        return copy(out if out is conv_b else out.at[h], into.at[ctx, h], ss.at[i, h], rs.at[ctx, h], (to, fsdp, batch))

    def send(out, into, ss, rs, h, sign, done):
        def act(c):
            c.wait_send() if done else c.start()

        if pair == 2:
            @pl.when(core == (0 if sign > 0 else 1))
            def _():
                act(sent(out, into, ss, rs, h, mate, 0))

        for i in range(1, n_ctx // pair):
            to = ctx + sign * pair * i

            @pl.when(jnp.logical_and(to >= 0, to < n_ctx))
            def _():
                act(sent(out, into, ss, rs, h, to, i))

    def passed(into, rs, ps, s, h):
        return copy(into.at[s, h], into.at[s, h], ps.at[s, h], rs.at[s, h], (mate, fsdp, batch))

    def relays(s, sign):
        if pair == 1:
            return s < 0
        there = s // pair < chip if sign > 0 else s // pair > chip
        return jnp.logical_and(there, core == s % pair)

    def receive(into, rs, ps, total, h, sign):
        for s in range(n_ctx):
            if pair == 2:
                @pl.when(relays(s, sign))
                def _():
                    passed(into, rs, ps, s, h).wait_recv()
                    passed(into, rs, ps, s, h).start()
        total[h] = jnp.zeros(total.shape[1:], f32)
        for s in range(n_ctx):
            wanted = s < ctx if sign > 0 else s > ctx
            plain = jnp.logical_and(wanted, jnp.logical_not(relays(s, sign))) if pair == 2 else wanted

            @pl.when(plain)
            def _():
                passed(into, rs, ps, s, h).wait_recv()

            @pl.when(wanted)
            def _():
                total[h] += into[s, h].astype(f32)

    def finish(out, into, ss, rs, ps, sign):
        for h in range(into.shape[1]):
            send(out, into, ss, rs, h, sign, True)
            if pair == 2:
                for s in range(n_ctx):
                    @pl.when(relays(s, sign))
                    def _():
                        passed(into, rs, ps, s, h).wait_send()

    @pl.when(inner)
    def _():
        vrim_copy().wait_recv()
        ext_v[0:RIM_V] = vrim_in[...].astype(f32)

    @pl.when(jnp.logical_not(inner))
    def _():
        ext_v[0:RIM_V] = jnp.zeros((RIM_V, wide), f32)

    ext_v[RIM_V:] = values[...].astype(f32)
    running = conv_v[0:1] * ext_v[RIM_V:]
    for j in range(1, CONV):
        running = running + conv_v[j : j + 1] * ext_v[RIM_V - j : RIM_V - j + positions]
    conv_b[...] = running.astype(bf16)
    if gather:
        send(conv_b, v_in, v_ss, v_rs, 0, 1, False)

    for r in range(1, n_fsdp):
        src = lax.rem(fsdp + r, n_fsdp)
        copy(part_in.at[src], part_in.at[src], part_ss.at[r], part_rs.at[src], (ctx, src, batch)).wait_recv()
    raw = part_f[fsdp]
    for r in range(1, n_fsdp):
        raw = raw + part_in[lax.rem(fsdp + r, n_fsdp)].astype(f32)
    raw = raw.astype(bf16).astype(f32)

    @pl.when(inner)
    def _():
        for s in range(n_fsdp):
            copy(rim_in.at[s], rim_in.at[s], rim_ss.at[s], rim_rs.at[s], (ctx - 1, s, batch)).wait_recv()
        rows = rim_in[0]
        for s in range(1, n_fsdp):
            rows = rows + rim_in[s]
        rows = rows.astype(bf16).astype(f32)
        block = jnp.concatenate([jnp.zeros((positions - RIM, rows.shape[1]), f32), rows], axis=0)
        rim_t[...] = block.T

    @pl.when(jnp.logical_not(inner))
    def _():
        rim_t[...] = jnp.zeros(rim_t.shape, f32)

    before = rim_t[pl.ds(pl.multiple_of(fsdp * width, width), width), :]
    lane = lax.broadcasted_iota(jnp.int32, (width, positions), 1)
    taps = [column_of(conv_qk[j : j + 1]) for j in range(CONV)]
    running = taps[0] * raw
    for j in range(1, CONV):
        moved = jnp.where(lane < j, pltpu.roll(before, j, 1), pltpu.roll(raw, j, 1))
        running = running + taps[j] * moved
    qk_t = running.astype(bf16).astype(f32)
    qk = qk_t.T.astype(bf16)

    q_t = [qk_t[h * 2 * F : h * 2 * F + F] for h in range(heads)]
    k_t = [qk_t[h * 2 * F + F : (h + 1) * 2 * F] for h in range(heads)]
    fk_t = [features(k) for k in k_t]

    def k_copy(r):
        return copy(k_out, k_in.at[ctx], k_ss.at[r], k_rs.at[ctx], (ctx + r, fsdp, batch))

    if gather:
        k_out[...] = qk_t.astype(bf16)
        for r in range(1, n_ctx):
            @pl.when(ctx + r < n_ctx)
            def _():
                k_copy(r).start()
        for i in range(n_ctx):
            if pair == 2:
                @pl.when(relays(i, 1))
                def _():
                    passed(v_in, v_rs, v_ps, i, 0).wait_recv()
                    passed(v_in, v_rs, v_ps, i, 0).start()
        x_start(1)
    for h in range(0 if gather else heads):
        state_out[h] = dot(fk_t[h].astype(bf16), conv_b[:, h * E : (h + 1) * E]).astype(bf16)
        send(state_out, state_in, state_ss, state_rs, h, 1, False)
    fq_t = [features(q) for q in q_t]
    fk = [x.T.astype(bf16) for x in fk_t]
    at_row = lax.broadcasted_iota(jnp.int32, (positions, positions), 0)
    at_col = lax.broadcasted_iota(jnp.int32, (positions, positions), 1)
    scores_t, kernels_t, local = [], [], []
    for h in range(heads):
        q, k = qk[:, h * 2 * F : h * 2 * F + F], qk[:, h * 2 * F + F : (h + 1) * 2 * F]
        score = dot(q, k_t[h].astype(bf16)) * F ** (-0.5)
        kernel = jnp.where(at_col <= at_row, 1.0 + score + 0.5 * score * score, 0.0).astype(bf16)
        local.append(dot(kernel, conv_b[:, h * E : (h + 1) * E]))
        score_t = dot(k, q_t[h].astype(bf16)) * F ** (-0.5)
        scores_t.append(score_t)
        kernels_t.append(
            jnp.where(at_row <= at_col, 1.0 + score_t + 0.5 * score_t * score_t, 0.0).astype(bf16)
        )

    def earlier(act):
        for i in range(n_ctx - 1):
            @pl.when(i < ctx)
            def _():
                for h in range(heads):
                    q = qk[:, h * 2 * F : h * 2 * F + F]
                    k = k_in[i, h * 2 * F + F : (h + 1) * 2 * F]
                    act(i, h, k, dot(q, k) * F ** (-0.5), v_in[i, 0, :, h * E : (h + 1) * E])

    def mix(i, h, k, score, value):
        kernel = (1.0 + score + 0.5 * score * score).astype(bf16)
        mixed_f[:, h * E : (h + 1) * E] += dot(kernel, value)

    def pull(i, h, k, score, value):
        d_kernel = dot_nt(mixed_b[:, h * E : (h + 1) * E], value)
        d_score = (d_kernel * (1.0 + score) * F ** (-0.5)).astype(bf16)
        pulled[h] += dot_nt(k, d_score)

    if gather:
        for h in range(heads):
            mixed_f[:, h * E : (h + 1) * E] = local[h]
        for i in range(n_ctx - 1):
            @pl.when(i < ctx)
            def _():
                copy(k_in.at[i], k_in.at[i], k_ss.at[i], k_rs.at[i], (i, fsdp, batch)).wait_recv()

            @pl.when(jnp.logical_and(i < ctx, jnp.logical_not(relays(i, 1))) if pair == 2 else i < ctx)
            def _():
                passed(v_in, v_rs, v_ps, i, 0).wait_recv()
        earlier(mix)

    prior_b = []
    for h in range(heads):
        lanes = slice(h * E, (h + 1) * E)
        if gather:
            mixed = mixed_f[:, lanes]
        else:
            receive(state_in, state_rs, pass_s, prior, h, 1)
            prior_b.append(prior[h].astype(bf16))
            mixed = local[h] + dot(fq_t[h].T.astype(bf16), prior_b[h])
        inv = lax.rsqrt(jnp.mean(mixed * mixed, axis=-1, keepdims=True) + eps_norm)
        normed = mixed * inv
        attended[:, lanes] = normed.astype(bf16)
        g = d_attn[:, lanes].astype(f32)
        d_mixed = (inv * (g - normed * jnp.mean(g * normed, axis=-1, keepdims=True))).astype(bf16)
        mixed_b[:, lanes] = d_mixed
        grad_out[h] = dot(fq_t[h].astype(bf16), d_mixed).astype(bf16)
        send(grad_out, grad_in, grad_ss, grad_rs, h, -1, False)

    d_q, d_k, d_v = [], [], []
    if gather:
        x_start(2)
        pulled[...] = jnp.zeros(pulled.shape, f32)
        earlier(pull)
    for h in range(heads):
        lanes = slice(h * E, (h + 1) * E)
        d_mixed, value = mixed_b[:, lanes], conv_b[:, lanes]
        d_kernel_t = dot_nt(value, d_mixed)
        d_score_t = jnp.where(
            at_row <= at_col, d_kernel_t * (1.0 + scores_t[h]), 0.0
        ) * F ** (-0.5)
        d_score_t = d_score_t.astype(bf16)
        d_q.append(
            dot(k_t[h].astype(bf16), d_score_t)
            + (pulled[h] if gather else features_back(q_t[h], dot_nt(prior_b[h], d_mixed)))
        )
        d_k.append(dot_nt(q_t[h].astype(bf16), d_score_t))
        d_v.append(dot(kernels_t[h], d_mixed))

    rows, later_b = [], []
    for h in range(heads):
        receive(grad_in, grad_rs, back_s, later, h, -1)
        later_b.append(later[h].astype(bf16))
        back = features_back(k_t[h], dot_nt(later_b[h], conv_b[:, h * E : (h + 1) * E]))
        rows += [d_q[h], d_k[h] + back]
    d_qk_t = jnp.concatenate(rows, axis=0)

    def dq_copy(r):
        peer = lax.rem(me + r, group)
        return copy(
            dq_all.at[me], dq_all.at[me], dq_ss.at[r], dq_rs.at[me],
            (peer // n_batch, fsdp, lax.rem(peer, n_batch)),
        )

    def dqk_copy():
        return copy(dqk_out, dqk_in, dqk_ss, dqk_rs, (ctx - 1, fsdp, batch))

    if gather:
        dq_all[me] = d_qk_t.astype(bf16)
        for r in range(1, group):
            dq_copy(r).start()
    else:
        dqk_out[...] = d_qk_t

        @pl.when(inner)
        def _():
            dqk_copy().start()

    def dv_copy():
        return copy(
            dv_ext.at[pl.ds(0, RIM)], dv_ext.at[pl.ds(positions, RIM)], dv_ss, dv_rs, (ctx - 1, fsdp, batch)
        )

    for h in range(heads):
        dv_ext[0:positions, h * E : (h + 1) * E] = d_v[h] + dot(fk[h], later_b[h])

    @pl.when(inner)
    def _():
        dv_copy().start()

    def convolve_back(here, after):
        running = taps[0] * here
        for j in range(1, CONV):
            moved = pltpu.roll(here, positions - j, 1)
            rim = 0.0 if after is None else pltpu.roll(after, positions - j, 1)
            running = running + taps[j] * jnp.where(lane >= positions - j, rim, moved)
        return running.astype(bf16)

    if not gather:
        @pl.when(outer)
        def _():
            dqk_copy().wait_recv()

        @pl.when(jnp.logical_not(outer))
        def _():
            dqk_in[...] = jnp.zeros(dqk_in.shape, f32)

        grad_w[...] = convolve_back(d_qk_t, dqk_in[...])

    @pl.when(outer)
    def _():
        dv_copy().wait_recv()

    @pl.when(jnp.logical_not(outer))
    def _():
        dv_ext[positions:] = jnp.zeros((RIM, wide), f32)

    running = conv_v[0:1] * dv_ext[0:positions]
    for j in range(1, CONV):
        running = running + conv_v[j : j + 1] * dv_ext[j : j + positions]
    grad_v[...] = running.astype(bf16)

    if gather:
        for r in range(1, group):
            src = lax.rem(me + r, group)
            to = (src // n_batch, fsdp, lax.rem(src, n_batch))
            copy(x_in.at[src], x_in.at[src], x_ss.at[r], x_rs.at[src], to).wait_recv()
            copy(dq_all.at[src], dq_all.at[src], dq_ss.at[r], dq_rs.at[src], to).wait_recv()
        blocks = [dq_all[s].astype(f32) for s in range(group)]
        d_pre = [
            convolve_back(blocks[s], blocks[s + n_batch] if s + n_batch < group else None)
            for s in range(group)
        ]
        total = dot(jnp.concatenate(d_pre, axis=1), x_in[...].reshape(group * positions, cols))
        grad_w[...] = total * float(positions * group) ** (-0.5)
        for r in range(1, group):
            x_copy(r).wait_send()
            dq_copy(r).wait_send()

    for r in range(1, n_fsdp):
        part_copy(r).wait_send()

    @pl.when(outer)
    def _():
        for r in range(n_fsdp):
            rim_copy(r).wait_send()
        vrim_copy().wait_send()

    @pl.when(inner)
    def _():
        if not gather:
            dqk_copy().wait_send()
        dv_copy().wait_send()

    if gather:
        finish(conv_b, v_in, v_ss, v_rs, v_ps, 1)
        for r in range(1, n_ctx):
            @pl.when(ctx + r < n_ctx)
            def _():
                k_copy(r).wait_send()
    else:
        finish(state_out, state_in, state_ss, state_rs, pass_s, 1)
    finish(grad_out, grad_in, grad_ss, grad_rs, back_s, -1)


def shards(dims, inputs, values, w_qk, conv_qk, conv_v, d_attn):
    n_ctx, n_fsdp, n_batch = dims
    tokens = inputs[0]
    positions, model = tokens.shape
    wide = values.shape[2]
    width = conv_qk.shape[1]
    heads = width // (2 * F)
    group = n_ctx * n_batch
    cols = model // group
    gather = cols % 128 == 0
    last = (width, cols) if gather else (width, positions)
    slots = group if gather else 1
    dma = pltpu.SemaphoreType.DMA
    state = (heads, PACKED, E)
    vmem = pl.BlockSpec(memory_space=pltpu.VMEM)
    hbm = pl.BlockSpec(memory_space=pl.ANY)
    scratch = [
        pltpu.VMEM(tokens.shape, bf16),
        pltpu.VMEM((positions, wide), bf16),
        pltpu.VMEM(w_qk.shape, bf16),
        pltpu.VMEM(conv_qk.shape, f32),
        pltpu.VMEM(conv_v.shape, f32),
        pltpu.VMEM((positions, wide), bf16),
        pltpu.VMEM((positions, w_qk.shape[0]), bf16),
        pltpu.VMEM((n_fsdp, width, positions), f32),
        pltpu.VMEM((n_fsdp, width, positions), bf16),
        pltpu.VMEM((n_fsdp, width, positions), bf16),
        pltpu.VMEM((RIM, w_qk.shape[1]), f32),
        pltpu.VMEM((n_fsdp, RIM, w_qk.shape[1]), f32),
        pltpu.VMEM((w_qk.shape[1], positions), f32),
        pltpu.VMEM((RIM_V, wide), bf16),
        pltpu.VMEM((RIM_V + positions, wide), f32),
        pltpu.VMEM((positions, wide), bf16),
        pltpu.VMEM(state, bf16),
        pltpu.VMEM((n_ctx,) + state, bf16),
        pltpu.VMEM(state, f32),
        pltpu.VMEM(state, bf16),
        pltpu.VMEM((n_ctx,) + state, bf16),
        pltpu.VMEM(state, f32),
        pltpu.VMEM((positions, wide), bf16),
        pltpu.VMEM((positions + RIM, wide), f32),
        pltpu.VMEM((width, positions), f32),
        pltpu.VMEM((width, positions), f32),
        pltpu.VMEM((slots, positions, cols if gather else 128), bf16),
        pltpu.VMEM((slots, width, positions), bf16),
        pltpu.VMEM((n_ctx, 1, positions, wide), bf16),
        pltpu.VMEM((width, positions), bf16),
        pltpu.VMEM((n_ctx, width, positions), bf16),
        pltpu.VMEM((positions, wide), f32),
        pltpu.VMEM((heads, F, positions), f32),
        dma((n_fsdp,)), dma((n_fsdp,)), dma((n_fsdp,)), dma((n_fsdp,)), dma, dma,
        dma((n_ctx, heads)), dma((n_ctx, heads)), dma((n_ctx, heads)), dma((n_ctx, heads)),
        dma, dma, dma, dma,
        dma((slots,)), dma((slots,)), dma((slots,)), dma((slots,)),
        dma((7,)), dma((n_ctx, heads)), dma((n_ctx, heads)),
        dma((n_ctx, 1)), dma((n_ctx, 1)), dma((n_ctx, 1)), dma((n_ctx,)), dma((n_ctx,)),
    ]
    place = pltpu.VMEM if gather else jax.ShapeDtypeStruct
    attended, grad_v, tail = pl.pallas_call(
        functools.partial(body, (n_ctx, n_fsdp, n_batch, gather)),
        out_shape=(
            place((positions, wide), bf16),
            place((positions, wide), bf16),
            place(last, f32 if gather else bf16),
        ),
        in_specs=[hbm] * 6,
        out_specs=(vmem,) * 3,
        scratch_shapes=scratch,
        compiler_params=pltpu.CompilerParams(
            collective_id=0, has_side_effects=True, vmem_limit_bytes=56 * 2**20
        ),
    )(tokens, values[0], w_qk, conv_qk, conv_v, d_attn[0])
    if gather:
        grad_w = tail.T
    else:
        grad_w = lax.psum_scatter(
            dot(tail, tokens).T, ("ctx", "batch"), scatter_dimension=0, tiled=True
        ) * float(positions * group) ** (-0.5)
    return (attended[None], grad_v[None], grad_w)


def solution(mesh):
    in_specs = (
        P("batch", "ctx", None),
        P("batch", "ctx", "fsdp"),
        P("fsdp", None),
        P(None, "fsdp"),
        P(None, "fsdp"),
        P("batch", "ctx", "fsdp"),
    )
    out_specs = (P("batch", "ctx", "fsdp"), P("batch", "ctx", "fsdp"), P(("ctx", "batch"), "fsdp"))
    dims = (mesh.shape["ctx"], mesh.shape["fsdp"], mesh.shape["batch"])
    return jax.shard_map(
        functools.partial(shards, dims), mesh=mesh, in_specs=in_specs, out_specs=out_specs, check_vma=False
    )
```
